128 devices in a mesh: img: 16 (over y, x_lo, core), ifg: 8 (over x_hi, z).
Axes of the slice: x: 4 (x_hi: 2, x_lo: 2; x = x_hi * 2 + x_lo), y: 4, z: 4, core: 2. Of those that a mesh axis runs over, the one named last changes fastest.
Arguments:
- phases: bfloat16 [1024, 8, 16384], P('ifg', None, 'img'), may hold values from -15 to 15
- coherence: bfloat16 [1024, 8, 16384], P('ifg', None, 'img'), may hold values from 0.099609375 to 1
- kernel_taps: float32 [3, 5], replicated, may hold values from 0.2 to 1
- inverse: bfloat16 [256, 1024], replicated, may hold values from -0.1875 to 0.1875
- date_pairs: int32 [1024, 2], replicated, may hold values from 0 to 255, as said below
- triplets: int32 [512, 3], replicated, may hold values from 0 to 1023
Outputs:
- displacement: bfloat16 [256, 8, 16384], P(None, None, ('img', 'ifg'))
- closure: bfloat16 [512, 8, 16384], P(None, None, ('img', 'ifg'))
The draws below stay inside these ranges and needn't reach their ends.
Inputs may be any that keep to these rules, and one draw needn't show every extreme that they name: `date_pairs`: each row holds the earlier date of an interferogram, then a strictly later one.
All inputs are finite; a program needn't handle non-finite values.
Results may differ from the reference program's by a relative error of at most 0.0055.
Values may be sent and summed in bfloat16 or wider, within the bound.
No kernel may reach another device: no remote copies, remote signals or barrier semaphores. Data moves between devices by JAX's collectives and lax.ppermute only.
A program may use at most 64 MiB of HBM per device.

```python
import math
import jax
import jax.numpy as jnp
from jax import lax

NIFG = 1024
NDATE = 256
NTRI = 512
ROWS = 8
RADIUS = 2
COLS_DEV = 1024
COLS = 16384


def draw_date_pairs(key, part):
    first_key = jax.random.fold_in(key, 11)
    second_key = jax.random.fold_in(key, 12)
    earlier_date = jax.random.randint(first_key, (NIFG,), 0, NDATE - 1)
    offset = jax.random.randint(second_key, (NIFG,), 0, NDATE - 1 - earlier_date)
    later_date = earlier_date + 1 + offset
    earlier_date = earlier_date.at[0].set(0)
    later_date = later_date.at[0].set(NDATE - 1)
    return jnp.stack([earlier_date, later_date], axis=1).astype(jnp.int32)


def plant(array, key, least, high):
    longest = array.shape.index(max(array.shape))
    spots = []
    for shift in (0, 1):
        where = [jax.random.randint(jax.random.fold_in(key, axis), (), 0, length) for axis, length in enumerate(array.shape)]
        where[longest] = (where[longest] + shift) % array.shape[longest]
        spots.append(tuple(where))
    return array.at[spots[0]].set(least).at[spots[1]].set(high)


def levels(stream_key, dims, pieces, low, largest):
    factor_of = 1.0
    for axis_at, shards_of in pieces:
        draws = jax.random.uniform(jax.random.fold_in(jax.random.fold_in(stream_key, 6), axis_at), (shards_of,), jnp.float32, low / len(pieces), largest / len(pieces))
        factor_of = factor_of * jnp.repeat(jnp.exp(draws), dims[axis_at] // shards_of).reshape((-1,) + (1,) * (len(dims) - 1 - axis_at))
    return factor_of


def noise(rng, dims, scale, most, shards=(), kind=jnp.bfloat16):
    loudness = levels(rng, dims, shards, -0.22, 0.18) if shards else 1.0
    array = jax.random.normal(rng, dims, jnp.float32) * scale * loudness
    return jnp.minimum(jnp.maximum(array, -most), most).astype(kind)


def setup_inputs(seed: int = 0) -> dict:
    keys = jax.random.split(jax.random.key(seed), 7)
    return {
        "phases": noise(keys[0], (NIFG, ROWS, COLS), 3.0, 15.0, ((0, 8), (2, 16))),
        "coherence": jnp.clip(0.099609375 + 0.9003906 * jax.random.uniform(keys[1], (NIFG, ROWS, COLS), jnp.float32) ** levels(keys[1], (NIFG, ROWS, COLS), ((0, 8), (2, 16)), -0.2, 0.2), 0.099609375, 1.0).astype(jnp.bfloat16),
        "kernel_taps": jnp.clip(jnp.exp(jax.random.uniform(keys[2], (3, 2 * RADIUS + 1), jnp.float32, math.log(0.2), math.log(1.0))), 0.2, 1.0),
        "inverse": noise(keys[3], (NDATE, NIFG), NIFG ** -0.5, 0.1875),
        "date_pairs": draw_date_pairs(jax.random.fold_in(keys[6], 71), 0),
        "triplets": plant(jax.random.randint(keys[5], (NTRI, 3), 0, NIFG), jax.random.fold_in(keys[5], 1), 0, NIFG - 1).astype(jnp.int32),
    }


def smooth_block(phase_block, coherence_block, kernel_taps):
    values = phase_block.astype(jnp.float32)
    weights = coherence_block.astype(jnp.float32)
    row_count = values.shape[1]
    col_count = values.shape[2]
    half_width = (kernel_taps.shape[1] - 1) // 2
    product = jnp.pad(values * weights, ((0, 0), (1, 1), (half_width, half_width)))
    padded_weights = jnp.pad(weights, ((0, 0), (1, 1), (half_width, half_width)))
    numerator = jnp.zeros(values.shape, jnp.float32)
    denominator = jnp.zeros(values.shape, jnp.float32)
    for row_shift in range(kernel_taps.shape[0]):
        for col_shift in range(kernel_taps.shape[1]):
            factor = kernel_taps[row_shift, col_shift]
            numerator = numerator + factor * product[:, row_shift:row_shift + row_count, col_shift:col_shift + col_count]
            denominator = denominator + factor * padded_weights[:, row_shift:row_shift + row_count, col_shift:col_shift + col_count]
    return (numerator / denominator).astype(jnp.bfloat16)


def invert_block(block, inverse, date_pairs, triplets):
    count_ifg, rows_here, width_here = block.shape
    flattened = block.reshape(count_ifg, rows_here * width_here)
    displacement = jnp.dot(inverse, flattened, preferred_element_type=jnp.float32).astype(jnp.bfloat16)
    later = jnp.take(displacement, date_pairs[:, 1], axis=0).astype(jnp.float32)
    earlier = jnp.take(displacement, date_pairs[:, 0], axis=0).astype(jnp.float32)
    misfit = flattened.astype(jnp.float32) - (later - earlier)
    closure = jnp.take(misfit, triplets[:, 0], axis=0) + jnp.take(misfit, triplets[:, 1], axis=0) - jnp.take(misfit, triplets[:, 2], axis=0)
    return (displacement.reshape(-1, rows_here, width_here), closure.astype(jnp.bfloat16).reshape(-1, rows_here, width_here))


def reference(phases, coherence, kernel_taps, inverse, date_pairs, triplets):
    group = min(64, NIFG)
    groups = NIFG // group
    phase_groups = phases.reshape(groups, group, ROWS, COLS)
    coherence_groups = coherence.reshape(groups, group, ROWS, COLS)
    filtered = lax.map(lambda pair_in: smooth_block(pair_in[0], pair_in[1], kernel_taps), (phase_groups, coherence_groups))
    filtered = filtered.reshape(NIFG, ROWS, COLS)
    blocks = COLS // COLS_DEV
    column_blocks = filtered.reshape(NIFG, ROWS, blocks, COLS_DEV).transpose(2, 0, 1, 3)
    displacement, closure = lax.map(lambda block: invert_block(block, inverse, date_pairs, triplets), column_blocks)
    displacement = displacement.transpose(1, 2, 0, 3).reshape(NDATE, ROWS, COLS)
    closure = closure.transpose(1, 2, 0, 3).reshape(NTRI, ROWS, COLS)
    return (displacement, closure)
```

```python
import functools

import jax
import jax.numpy as jnp
from jax import lax
from jax.experimental import pallas as pl
from jax.experimental.pallas import tpu as pltpu
from jax.sharding import PartitionSpec as P

LANES = 128
F32 = jnp.float32
BF16 = jnp.bfloat16
VMEM = pl.BlockSpec(memory_space=pltpu.VMEM)
SMEM = pl.BlockSpec(memory_space=pltpu.SMEM)
ANY = pl.BlockSpec(memory_space=pl.ANY)
ORDER = (4, 2, 5, 7, 6, 1, 3)
EARLY = (0, 4, 2, 5, 7, 1)
LATE = (6, 3)


def cost(flops, nbytes):
    return pl.CostEstimate(flops=int(flops), bytes_accessed=int(nbytes), transcendentals=0)


def params(mib=48):
    return pltpu.CompilerParams(vmem_limit_bytes=mib * 1024 * 1024)


def pack_kernel(first_phase, last_phase, first_coh, last_coh, left_out, right_out):
    lane = lax.broadcasted_iota(jnp.int32, (4, 8, LANES), 2)
    to_left = jnp.zeros((4, 8, LANES), F32)
    to_right = jnp.zeros((4, 8, LANES), F32)
    for k in range(32):
        a = first_phase[:, k].astype(F32)
        b = first_coh[:, k].astype(F32)
        both = jnp.where(lane < 2, a, pltpu.roll(b, 2, 2))
        here = (lane >> 2) == k
        to_left = jnp.where(here, pltpu.roll(both, 4 * k, 2) if k else both, to_left)
        a = last_phase[:, k].astype(F32)
        b = last_coh[:, k].astype(F32)
        both = jnp.where(lane >= 126, b, pltpu.roll(a, 126, 2))
        shift = (4 * k + 4) % LANES
        to_right = jnp.where(here, pltpu.roll(both, shift, 2) if shift else both, to_right)
    left_out[...] = to_left.astype(BF16)
    right_out[...] = to_right.astype(BF16)


def pack_edges(phases, coherence):
    count, rows, width = phases.shape
    shape = (4, count // 4, rows, width)
    first = pl.BlockSpec((4, count // 4, rows, LANES), lambda i: (0, 0, 0, 0))
    last = pl.BlockSpec((4, count // 4, rows, LANES), lambda i: (0, 0, 0, width // LANES - 1))
    small = jax.ShapeDtypeStruct((4, rows, LANES), BF16)
    phase4 = phases.reshape(shape)
    coh4 = coherence.reshape(shape)
    return pl.pallas_call(
        pack_kernel,
        grid=(1,),
        in_specs=[first, last, first, last],
        out_specs=[pl.BlockSpec((4, rows, LANES), lambda i: (0, 0, 0))] * 2,
        out_shape=[small, small],
        compiler_params=params(),
        cost_estimate=cost(3e8, 2e6),
        name="pack_edges",
    )(phase4, phase4, coh4, coh4)


def filter_kernel(step, me_ref, taps_ref, phase_ref, coh_ref, left_ref, right_ref, out_ref, scratch):
    block = me_ref[0] ^ step
    count = phase_ref.shape[0]
    blocks = phase_ref.shape[2] // LANES
    taps = [[taps_ref[a, b] for b in range(5)] for a in range(3)]
    group = 2
    lane = lax.broadcasted_iota(jnp.int32, (group, 8, LANES), 2)
    row = lax.broadcasted_iota(jnp.int32, (group, 8, LANES), 1)

    def column(index):
        return pl.ds(pl.multiple_of(index * LANES, LANES), LANES)

    def one(i, left_edge, right_edge):
        at = pl.ds(i * group, group)
        centre = column(block)
        phase = phase_ref[at, :, centre].astype(F32)
        coh = coh_ref[at, :, centre].astype(F32)
        if left_edge or right_edge:
            packed = []
            ref = left_ref if left_edge else right_ref
            for j in range(group):
                which = i * group + j
                g = which // 32
                k = which % 32
                vector = ref[pl.ds(g, 1)].astype(F32)
                packed.append(pltpu.roll(vector, (LANES - 4 * k) % LANES, 2))
            packed = jnp.concatenate(packed, axis=0)
        if left_edge:
            phase_before = pltpu.roll(packed, 126, 2)
            coh_before = pltpu.roll(packed, 124, 2)
        else:
            phase_before = phase_ref[at, :, column(jnp.maximum(block - 1, 0))].astype(F32)
            coh_before = coh_ref[at, :, column(jnp.maximum(block - 1, 0))].astype(F32)
        if right_edge:
            phase_after = packed
            coh_after = pltpu.roll(packed, 126, 2)
        else:
            phase_after = phase_ref[at, :, column(jnp.minimum(block + 1, blocks - 1))].astype(F32)
            coh_after = coh_ref[at, :, column(jnp.minimum(block + 1, blocks - 1))].astype(F32)

        def shifted(before, here, after, offset):
            if offset == 0:
                return here
            if offset < 0:
                return pltpu.roll(jnp.where(lane >= LANES + offset, before, here), -offset, 2)
            return pltpu.roll(jnp.where(lane < offset, after, here), LANES - offset, 2)

        num = [None] * 3
        den = [None] * 3
        for b in range(5):
            weight = shifted(coh_before, coh, coh_after, b - 2)
            value = shifted(phase_before, phase, phase_after, b - 2) * weight
            for a in range(3):
                n = value * taps[a][b]
                d = weight * taps[a][b]
                num[a] = n if num[a] is None else num[a] + n
                den[a] = d if den[a] is None else den[a] + d

        def vertical(parts):
            down = jnp.where(row == 0, 0.0, pltpu.roll(parts[0], 1, 1))
            up = jnp.where(row == 7, 0.0, pltpu.roll(parts[2], 7, 1))
            return parts[1] + down + up

        bottom = vertical(den)
        inverse = pl.reciprocal(bottom, approx=True)
        inverse = inverse * (2.0 - bottom * inverse)
        inverse = inverse * (2.0 - bottom * inverse)
        result = vertical(num) * inverse
        scratch[pl.ds(pl.multiple_of(i * group * 8, group * 8), group * 8), :] = result.reshape(group * 8, LANES)

    def run(left_edge, right_edge):
        def body(i, carry):
            one(i, left_edge, right_edge)
            return carry

        lax.fori_loop(0, count // group, body, 0, unroll=2)

    @pl.when(block == 0)
    def _():
        run(True, False)

    @pl.when(block == blocks - 1)
    def _():
        run(False, True)

    @pl.when((block > 0) & (block < blocks - 1))
    def _():
        run(False, False)

    for r in range(8):
        out_ref[:, r * LANES : (r + 1) * LANES] = scratch[pl.ds(r, count, stride=8), :].astype(BF16)


def filter_block(step, me, taps, phases, coherence, left, right):
    count, rows, _ = phases.shape
    return pl.pallas_call(
        functools.partial(filter_kernel, step),
        in_specs=[SMEM, SMEM, VMEM, VMEM, VMEM, VMEM],
        out_specs=VMEM,
        out_shape=jax.ShapeDtypeStruct((count, rows * LANES), BF16),
        scratch_shapes=[pltpu.VMEM((count * rows, LANES), F32)],
        compiler_params=params(),
        cost_estimate=cost(1.5e9, 1e6),
        name="filter",
    )(me, taps, phases, coherence, left, right)


def network_kernel(pairs_ref, triplets_ref, member_ref, dates_ref, first):
    count = pairs_ref.shape[1]
    triplet_count = triplets_ref.shape[1]
    date_count = dates_ref.shape[1]
    pairs = jnp.concatenate([pairs_ref[...], jnp.zeros((6, count), jnp.int32)], axis=0).T
    triplets = jnp.concatenate([triplets_ref[...], jnp.zeros((5, triplet_count), jnp.int32)], axis=0).T
    for at in range(0, count, LANES):
        column = lax.broadcasted_iota(jnp.int32, (LANES, date_count), 1)
        block = pairs[at : at + LANES]
        value = jnp.where(column == block[:, 1:2], 1.0, 0.0) - jnp.where(column == block[:, 0:1], 1.0, 0.0)
        first[at : at + LANES, :] = value.astype(BF16)
    for at in range(0, triplet_count, LANES):
        column = lax.broadcasted_iota(jnp.int32, (LANES, count), 1)
        block = triplets[at : at + LANES]
        value = (
            jnp.where(column == block[:, 0:1], 1.0, 0.0)
            + jnp.where(column == block[:, 1:2], 1.0, 0.0)
            - jnp.where(column == block[:, 2:3], 1.0, 0.0)
        )
        member_ref[at : at + LANES, :] = value.astype(BF16)
    dates_ref[...] = jnp.dot(member_ref[...], first[...], preferred_element_type=F32).astype(BF16)


def network(date_pairs, triplets, dates):
    count = date_pairs.shape[0]
    triplet_count = triplets.shape[0]
    return pl.pallas_call(
        network_kernel,
        in_specs=[VMEM, VMEM],
        out_specs=[VMEM, VMEM],
        out_shape=[
            jax.ShapeDtypeStruct((triplet_count, count), BF16),
            jax.ShapeDtypeStruct((triplet_count, dates), BF16),
        ],
        scratch_shapes=[pltpu.VMEM((count, dates), BF16)],
        compiler_params=params(),
        cost_estimate=cost(2e9, 1e6),
        name="network",
    )(date_pairs.T, triplets.T)


def piece(me, step, matrix_ref, rows, share):
    source = pl.multiple_of((me ^ step) * share, share)
    return matrix_ref[rows, pl.ds(source, share)]


def early_kernel(steps, me_ref, inverse_ref, member_ref, *refs):
    pieces, total_ref = refs[:-1], refs[-1]
    me = me_ref[0]
    share = pieces[0].shape[0]
    dates = inverse_ref.shape[0]
    for at in range(0, total_ref.shape[0], dates):
        matrix_ref, rows = (inverse_ref, pl.ds(0, dates)) if at == 0 else (member_ref, pl.ds(at - dates, dates))
        total = None
        for j in range(0, len(steps), 2):
            left = jnp.concatenate([piece(me, s, matrix_ref, rows, share) for s in steps[j : j + 2]], axis=1)
            right = jnp.concatenate([p[...] for p in pieces[j : j + 2]], axis=0)
            part = jnp.dot(left, right, preferred_element_type=F32)
            total = part if total is None else total + part
        total_ref[pl.ds(at, dates), :] = total


def early_sum(steps, me, inverse, member, pieces):
    rows = inverse.shape[0] + member.shape[0]
    width = pieces[0].shape[1]
    return pl.pallas_call(
        functools.partial(early_kernel, steps),
        in_specs=[SMEM] + [VMEM] * (2 + len(pieces)),
        out_specs=VMEM,
        out_shape=jax.ShapeDtypeStruct((rows, width), F32),
        compiler_params=params(),
        cost_estimate=cost(2e9, 1e6),
        name="early_sum",
    )(me, inverse, member, *pieces)


def late_kernel(steps, me_ref, inverse_ref, member_ref, dates_ref, total_ref, *refs):
    count = len(steps)
    pieces = refs[:count]
    disp_hbm, closure_hbm, disp, closure, rounded, spread, sems = refs[count:]
    me = me_ref[0]
    share = pieces[0].shape[0]
    dates = inverse_ref.shape[0]
    rows = disp.shape[1]
    right = jnp.concatenate([p[...] for p in pieces], axis=0)
    chunk = 128

    def times(matrix_ref, at):
        left = jnp.concatenate([piece(me, s, matrix_ref, pl.ds(at, chunk), share) for s in steps], axis=1)
        return jnp.dot(left, right, preferred_element_type=F32)

    def regroup(slot, value, out, at):
        for r in range(rows):
            spread[slot, pl.ds(r, chunk, stride=rows), :] = value[:, r * LANES : (r + 1) * LANES]
        out[pl.ds(at, chunk)] = spread[slot].reshape(chunk, rows, LANES).astype(BF16)

    copies = []

    def send(out, hbm, at):
        copy = pltpu.make_async_copy(out.at[pl.ds(at, chunk)], hbm.at[pl.ds(at, chunk)], sems.at[len(copies)])
        copy.start()
        copies.append(copy)

    for at in range(0, dates, chunk):
        value = (total_ref[pl.ds(at, chunk), :] + times(inverse_ref, at)).astype(BF16)
        rounded[pl.ds(at, chunk), :] = value
        regroup(len(copies) % 2, value.astype(F32), disp, at)
        send(disp, disp_hbm, at)
    for at in range(0, closure.shape[0], chunk):
        value = total_ref[pl.ds(dates + at, chunk), :] + times(member_ref, at)
        value = value - jnp.dot(dates_ref[pl.ds(at, chunk), :], rounded[...], preferred_element_type=F32)
        regroup(len(copies) % 2, value, closure, at)
        send(closure, closure_hbm, at)
    for copy in copies:
        copy.wait()


def late_sum(steps, me, inverse, member, dates_matrix, total, pieces, rows):
    dates = inverse.shape[0]
    triplet_count = member.shape[0]
    width = pieces[0].shape[1]
    outs = [(dates, rows, LANES), (triplet_count, rows, LANES)]
    return pl.pallas_call(
        functools.partial(late_kernel, steps),
        in_specs=[SMEM] + [VMEM] * (4 + len(pieces)),
        out_specs=[ANY, ANY],
        out_shape=[jax.ShapeDtypeStruct(shape, BF16) for shape in outs],
        scratch_shapes=[
            pltpu.VMEM(outs[0], BF16),
            pltpu.VMEM(outs[1], BF16),
            pltpu.VMEM((dates, width), BF16),
            pltpu.VMEM((2, 128 * rows, LANES), F32),
            pltpu.SemaphoreType.DMA(((dates + triplet_count) // 128,)),
        ],
        compiler_params=params(),
        cost_estimate=cost(3e9, 2e6),
        name="late_sum",
    )(me, inverse, member, dates_matrix, total, *pieces)


def per_device(phases, coherence, kernel_taps, inverse, date_pairs, triplets):
    rows = phases.shape[1]
    size = lax.axis_size("img")
    peers = lax.axis_size("ifg")
    me = lax.axis_index("ifg").astype(jnp.int32).reshape(1)
    to_left, to_right = pack_edges(phases, coherence)
    left = lax.ppermute(to_right, "img", [(i, i + 1) for i in range(size - 1)])
    right = lax.ppermute(to_left, "img", [(i + 1, i) for i in range(size - 1)])
    member, dates_matrix = network(date_pairs, triplets, inverse.shape[0])
    pieces = {}
    for step in ORDER:
        block = filter_block(step, me, kernel_taps, phases, coherence, left, right)
        pieces[step] = lax.ppermute(block, "ifg", [(i, i ^ step) for i in range(peers)])
    pieces[0] = filter_block(0, me, kernel_taps, phases, coherence, left, right)
    total = early_sum(EARLY, me, inverse, member, [pieces[s] for s in EARLY])
    return tuple(late_sum(LATE, me, inverse, member, dates_matrix, total, [pieces[s] for s in LATE], rows))


def solution(mesh):
    return jax.shard_map(
        per_device,
        mesh=mesh,
        in_specs=(P("ifg", None, "img"), P("ifg", None, "img"), P(), P(), P(), P()),
        out_specs=(P(None, None, ("img", "ifg")), P(None, None, ("img", "ifg"))),
        check_vma=False,
    )
```

```python
import functools

import jax
import jax.numpy as jnp
from jax import lax
from jax.experimental import pallas as pl
from jax.experimental.pallas import tpu as pltpu
from jax.sharding import PartitionSpec as P

LANES = 128
F32 = jnp.float32
BF16 = jnp.bfloat16
VMEM = pl.BlockSpec(memory_space=pltpu.VMEM)
SMEM = pl.BlockSpec(memory_space=pltpu.SMEM)
HBM = pl.BlockSpec(memory_space=pltpu.HBM)
SIZE = 1024
ORDER = (4, 2, 5, 7, 6, 1, 3)
EARLY = (0, 4, 2, 5, 7, 1)
LATE = (6, 3)


def cost(flops, nbytes):
    return pl.CostEstimate(flops=int(flops), bytes_accessed=int(nbytes), transcendentals=0)


def params(mib=16):
    return pltpu.CompilerParams(vmem_limit_bytes=mib * 1024 * 1024)


def pack_kernel(phase_hbm, coh_hbm, left_out, right_out, edges, sems):
    width = phase_hbm.shape[2]
    copies = []
    for j, hbm in enumerate((phase_hbm, coh_hbm)):
        for side, at in ((0, 0), (1, width - LANES)):
            copies.append(pltpu.make_async_copy(hbm.at[:, :, pl.ds(at, LANES)], edges.at[j, side], sems.at[2 * j + side]))
    for copy in copies:
        copy.start()
    lane = lax.broadcasted_iota(jnp.int32, (8, LANES), 1)
    for j in range(2):
        for side, out in ((0, left_out), (1, right_out)):
            copies[2 * j + side].wait()
            for g in range(4):
                packed = jnp.zeros((8, LANES), F32)
                for k in range(32):
                    value = edges[j, side, 32 * g + k].astype(F32)
                    value = pltpu.roll(value, 4 * k, 1) if k else value
                    first = 4 * k if side == 0 else (4 * k - 2) % LANES
                    packed = jnp.where((lane == first) | (lane == first + 1), value, packed)
                out[j, g] = packed.astype(BF16)


def pack_edges(phases, coherence):
    count, rows, _ = phases.shape
    small = jax.ShapeDtypeStruct((2, count // 32, rows, LANES), BF16)
    return pl.pallas_call(
        pack_kernel,
        in_specs=[HBM, HBM],
        out_specs=[VMEM, VMEM],
        out_shape=[small, small],
        scratch_shapes=[pltpu.VMEM((2, 2, count, rows, LANES), BF16), pltpu.SemaphoreType.DMA((4,))],
        compiler_params=params(60),
        cost_estimate=cost(3e8, 1e6),
        name="pack_edges",
    )(phases, coherence)


def bands_kernel(taps_ref, high_ref, low_ref):
    place = lax.broadcasted_iota(jnp.int32, (2 * LANES, LANES), 0)
    place = jnp.where(place >= LANES + 64, place - 2 * LANES, place)
    tap = place - lax.broadcasted_iota(jnp.int32, (2 * LANES, LANES), 1) + 2
    for a in range(3):
        band = jnp.zeros((2 * LANES, LANES), F32)
        for b in range(5):
            band = jnp.where(tap == b, taps_ref[a, b], band)
        high = band.astype(BF16)
        high_ref[:, a * LANES : (a + 1) * LANES] = high
        low_ref[:, a * LANES : (a + 1) * LANES] = (band - high.astype(F32)).astype(BF16)

def bands(taps):
    shape = jax.ShapeDtypeStruct((2 * LANES, 3 * LANES), BF16)
    return pl.pallas_call(bands_kernel, in_specs=[SMEM], out_specs=[VMEM, VMEM], out_shape=[shape, shape],
        compiler_params=params(), cost_estimate=cost(3e8, 1e5), name="bands")(taps)


def expand_kernel(left_ref, right_ref, phase_out, coh_out):
    lane = lax.broadcasted_iota(jnp.int32, (4, 8, LANES), 2)
    from_left = (lane & 3) >= 2
    for j, out in ((0, phase_out), (1, coh_out)):
        both = jnp.where(from_left, left_ref[j].astype(F32), right_ref[j].astype(F32))
        for k in range(32):
            out[:, k] = (pltpu.roll(both, (LANES - 4 * k) % LANES, 2) if k else both).astype(BF16)

def expand(left, right):
    shape = jax.ShapeDtypeStruct((4, 32, 8, LANES), BF16)
    out = pl.pallas_call(expand_kernel, in_specs=[VMEM, VMEM], out_specs=[VMEM, VMEM], out_shape=[shape, shape],
        compiler_params=params(), cost_estimate=cost(5e8, 1e5), name="expand")(left, right)
    return [o.reshape(128, 8, LANES) for o in out]


def filter_kernel(step, m, me_ref, high_ref, low_ref, phase_ref, coh_ref, phase_edge_ref, coh_edge_ref, out_ref, scratch):
    block = me_ref[0] ^ step
    count = phase_ref.shape[0]
    blocks = phase_ref.shape[2] // LANES
    group = m // 8
    lane = lax.broadcasted_iota(jnp.int32, (1, 1, LANES), 2)
    left_here = jnp.where(block == 0, LANES, 64)
    right_here = jnp.where(block == blocks - 1, 0, 64)
    use_left = lane >= left_here
    use_right = lane < right_here
    row = lax.broadcasted_iota(jnp.int32, (group, 8, LANES), 1)

    def column(index):
        return pl.ds(pl.multiple_of(index * LANES, LANES), LANES)
    here, before, after = column(block), column(jnp.maximum(block - 1, 0)), column(jnp.minimum(block + 1, blocks - 1))

    def body(i, carry):
        at = pl.ds(i * group, group)
        def edge(ref, edge_ref):
            return jnp.where(use_left, ref[at, :, before], jnp.where(use_right, ref[at, :, after], edge_ref[at]))
        def flat(x):
            return x.reshape(m, LANES)
        phase = jnp.concatenate([flat(phase_ref[at, :, here]), flat(edge(phase_ref, phase_edge_ref))], axis=1)
        coh = jnp.concatenate([flat(coh_ref[at, :, here]), flat(edge(coh_ref, coh_edge_ref))], axis=1)
        product = phase.astype(F32) * coh.astype(F32)
        major = product.astype(BF16)
        minor = (product - major.astype(F32)).astype(BF16)
        high, low = high_ref[...], low_ref[...]
        den = jnp.dot(jnp.concatenate([coh, coh], axis=1), jnp.concatenate([high, low], axis=0), preferred_element_type=F32)
        num = jnp.dot(jnp.concatenate([major, minor, major], axis=1), jnp.concatenate([high, high, low], axis=0), preferred_element_type=F32)
        def vertical(parts):
            p = [parts[:, a * LANES : (a + 1) * LANES].reshape(group, 8, LANES) for a in range(3)]
            down = jnp.where(row == 0, 0.0, pltpu.roll(p[0], 1, 1))
            up = jnp.where(row == 7, 0.0, pltpu.roll(p[2], 7, 1))
            return p[1] + down + up
        bottom = vertical(den)
        inverse = pl.reciprocal(bottom, approx=True)
        inverse = inverse * (2.0 - bottom * inverse)
        result = vertical(num) * inverse
        scratch[pl.ds(pl.multiple_of(i * m, m), m), :] = result.reshape(m, LANES)
        return carry
    if count // group == 1:
        body(0, 0)
    else:
        lax.fori_loop(0, count // group, body, 0)
    for r in range(8):
        out_ref[:, r * LANES : (r + 1) * LANES] = scratch[pl.ds(r, count, stride=8), :].astype(BF16)

def filter_block(step, me, bands, phases, coherence, phase_edge, coh_edge):
    count, rows, _ = phases.shape
    return pl.pallas_call(
        functools.partial(filter_kernel, step, SIZE),
        in_specs=[SMEM] + [VMEM] * 6,
        out_specs=VMEM,
        out_shape=jax.ShapeDtypeStruct((count, rows * LANES), BF16),
        scratch_shapes=[pltpu.VMEM((count * rows, LANES), F32)],
        compiler_params=params(),
        cost_estimate=cost(1.5e9, 1e6),
        name="filter",
    )(me, *bands, phases, coherence, phase_edge, coh_edge)


def network_kernel(pairs_ref, triplets_ref, member_ref, dates_ref, first):
    count = pairs_ref.shape[1]
    triplet_count = triplets_ref.shape[1]
    date_count = dates_ref.shape[1]
    pairs = jnp.concatenate([pairs_ref[...], jnp.zeros((6, count), jnp.int32)], axis=0).T
    triplets = jnp.concatenate([triplets_ref[...], jnp.zeros((5, triplet_count), jnp.int32)], axis=0).T
    for at in range(0, count, LANES):
        column = lax.broadcasted_iota(jnp.int32, (LANES, date_count), 1)
        block = pairs[at : at + LANES]
        value = jnp.where(column == block[:, 1:2], 1.0, 0.0) - jnp.where(column == block[:, 0:1], 1.0, 0.0)
        first[at : at + LANES, :] = value.astype(BF16)
    for at in range(0, triplet_count, LANES):
        column = lax.broadcasted_iota(jnp.int32, (LANES, count), 1)
        block = triplets[at : at + LANES]
        value = (
            jnp.where(column == block[:, 0:1], 1.0, 0.0)
            + jnp.where(column == block[:, 1:2], 1.0, 0.0)
            - jnp.where(column == block[:, 2:3], 1.0, 0.0)
        )
        member_ref[at : at + LANES, :] = value.astype(BF16)
    dates_ref[...] = jnp.dot(member_ref[...], first[...], preferred_element_type=F32).astype(BF16)


def network(date_pairs, triplets, dates):
    count = date_pairs.shape[0]
    triplet_count = triplets.shape[0]
    return pl.pallas_call(
        network_kernel,
        in_specs=[VMEM, VMEM],
        out_specs=[VMEM, VMEM],
        out_shape=[
            jax.ShapeDtypeStruct((triplet_count, count), BF16),
            jax.ShapeDtypeStruct((triplet_count, dates), BF16),
        ],
        scratch_shapes=[pltpu.VMEM((count, dates), BF16)],
        compiler_params=params(),
        cost_estimate=cost(2e9, 1e6),
        name="network",
    )(date_pairs.T, triplets.T)


def piece(me, step, matrix_ref, rows, share):
    source = pl.multiple_of((me ^ step) * share, share)
    return matrix_ref[rows, pl.ds(source, share)]


def early_kernel(steps, me_ref, inverse_ref, member_ref, *refs):
    pieces, total_ref = refs[:-1], refs[-1]
    me = me_ref[0]
    share = pieces[0].shape[0]
    dates = inverse_ref.shape[0]
    for at in range(0, total_ref.shape[0], dates):
        matrix_ref, rows = (inverse_ref, pl.ds(0, dates)) if at == 0 else (member_ref, pl.ds(at - dates, dates))
        total = None
        for j in range(0, len(steps), 2):
            left = jnp.concatenate([piece(me, s, matrix_ref, rows, share) for s in steps[j : j + 2]], axis=1)
            right = jnp.concatenate([p[...] for p in pieces[j : j + 2]], axis=0)
            part = jnp.dot(left, right, preferred_element_type=F32)
            total = part if total is None else total + part
        total_ref[pl.ds(at, dates), :] = total


def early_sum(steps, me, inverse, member, pieces):
    rows = inverse.shape[0] + member.shape[0]
    width = pieces[0].shape[1]
    return pl.pallas_call(
        functools.partial(early_kernel, steps),
        in_specs=[SMEM] + [VMEM] * (2 + len(pieces)),
        out_specs=VMEM,
        out_shape=jax.ShapeDtypeStruct((rows, width), F32),
        compiler_params=params(),
        cost_estimate=cost(2e9, 1e6),
        name="early_sum",
    )(me, inverse, member, *pieces)


def late_kernel(steps, me_ref, inverse_ref, member_ref, dates_ref, total_ref, *refs):
    count = len(steps)
    pieces = refs[:count]
    disp_hbm, closure_hbm, disp, closure, rounded, spread, sems = refs[count:]
    me = me_ref[0]
    share = pieces[0].shape[0]
    dates = inverse_ref.shape[0]
    rows = disp.shape[1]
    right = jnp.concatenate([p[...] for p in pieces], axis=0)
    chunk = 128

    def times(matrix_ref, at):
        left = jnp.concatenate([piece(me, s, matrix_ref, pl.ds(at, chunk), share) for s in steps], axis=1)
        return jnp.dot(left, right, preferred_element_type=F32)

    def regroup(slot, value, out, at):
        for r in range(rows):
            spread[slot, pl.ds(r, chunk, stride=rows), :] = value[:, r * LANES : (r + 1) * LANES]
        out[pl.ds(at, chunk)] = spread[slot].reshape(chunk, rows, LANES).astype(BF16)

    copies = []

    def send(out, hbm, at):
        copy = pltpu.make_async_copy(out.at[pl.ds(at, chunk)], hbm.at[pl.ds(at, chunk)], sems.at[len(copies)])
        copy.start()
        copies.append(copy)

    for at in range(0, dates, chunk):
        value = (total_ref[pl.ds(at, chunk), :] + times(inverse_ref, at)).astype(BF16)
        rounded[pl.ds(at, chunk), :] = value
        regroup(len(copies) % 2, value.astype(F32), disp, at)
        send(disp, disp_hbm, at)
    for at in range(0, closure.shape[0], chunk):
        value = total_ref[pl.ds(dates + at, chunk), :] + times(member_ref, at)
        value = value - jnp.dot(dates_ref[pl.ds(at, chunk), :], rounded[...], preferred_element_type=F32)
        regroup(len(copies) % 2, value, closure, at)
        send(closure, closure_hbm, at)
    for copy in copies:
        copy.wait()


def late_sum(steps, me, inverse, member, dates_matrix, total, pieces, rows):
    dates = inverse.shape[0]
    triplet_count = member.shape[0]
    width = pieces[0].shape[1]
    outs = [(dates, rows, LANES), (triplet_count, rows, LANES)]
    return pl.pallas_call(
        functools.partial(late_kernel, steps),
        in_specs=[SMEM] + [VMEM] * (4 + len(pieces)),
        out_specs=[HBM, HBM],
        out_shape=[jax.ShapeDtypeStruct(shape, BF16) for shape in outs],
        scratch_shapes=[
            pltpu.VMEM(outs[0], BF16),
            pltpu.VMEM(outs[1], BF16),
            pltpu.VMEM((dates, width), BF16),
            pltpu.VMEM((2, 128 * rows, LANES), F32),
            pltpu.SemaphoreType.DMA(((dates + triplet_count) // 128,)),
        ],
        compiler_params=params(),
        cost_estimate=cost(3e9, 2e6),
        name="late_sum",
    )(me, inverse, member, dates_matrix, total, *pieces)


def per_device(phases, coherence, kernel_taps, inverse, date_pairs, triplets):
    rows = phases.shape[1]
    size = lax.axis_size("img")
    peers = lax.axis_size("ifg")
    me = lax.axis_index("ifg").astype(jnp.int32).reshape(1)
    to_left, to_right = pack_edges(phases, coherence)
    left = lax.ppermute(to_right, "img", [(i, i + 1) for i in range(size - 1)])
    right = lax.ppermute(to_left, "img", [(i + 1, i) for i in range(size - 1)])
    tap_bands = bands(kernel_taps)
    member, dates_matrix = network(date_pairs, triplets, inverse.shape[0])
    edges = expand(left, right)
    pieces = {}
    for step in ORDER:
        block = filter_block(step, me, tap_bands, phases, coherence, *edges)
        pieces[step] = lax.ppermute(block, "ifg", [(i, i ^ step) for i in range(peers)])
    pieces[0] = filter_block(0, me, tap_bands, phases, coherence, *edges)
    total = early_sum(EARLY, me, inverse, member, [pieces[s] for s in EARLY])
    return tuple(late_sum(LATE, me, inverse, member, dates_matrix, total, [pieces[s] for s in LATE], rows))


def solution(mesh):
    return jax.shard_map(
        per_device,
        mesh=mesh,
        in_specs=(P("ifg", None, "img"), P("ifg", None, "img"), P(), P(), P(), P()),
        out_specs=(P(None, None, ("img", "ifg")), P(None, None, ("img", "ifg"))),
        check_vma=False,
    )
```

```python
import functools

import jax
import jax.numpy as jnp
from jax import lax
from jax.experimental import pallas as pl
from jax.experimental.pallas import tpu as pltpu
from jax.sharding import PartitionSpec as P

LANES = 128
F32 = jnp.float32
BF16 = jnp.bfloat16
VMEM = pl.BlockSpec(memory_space=pltpu.VMEM)
SMEM = pl.BlockSpec(memory_space=pltpu.SMEM)
HBM = pl.BlockSpec(memory_space=pltpu.HBM)
ANY = pl.BlockSpec(memory_space=pl.ANY)
SIZE = 1024
ORDER = (4, 2, 5, 7, 6, 1, 3)
EARLY = (0, 4, 2, 5, 7, 1)
LATE = (6, 3)


def cost(flops, nbytes):
    return pl.CostEstimate(flops=int(flops), bytes_accessed=int(nbytes), transcendentals=0)


def params(mib=16):
    return pltpu.CompilerParams(vmem_limit_bytes=mib * 1024 * 1024)


def pack_kernel(phase_hbm, coh_hbm, left_out, right_out, edges, sems):
    width = phase_hbm.shape[2]
    copies = []
    for j, hbm in enumerate((phase_hbm, coh_hbm)):
        for side, at in ((0, 0), (1, width - LANES)):
            copies.append(pltpu.make_async_copy(hbm.at[:, :, pl.ds(at, LANES)], edges.at[j, side], sems.at[2 * j + side]))
    for copy in copies:
        copy.start()
    lane = lax.broadcasted_iota(jnp.int32, (8, LANES), 1)
    for j in range(2):
        for side, out in ((0, left_out), (1, right_out)):
            copies[2 * j + side].wait()
            for g in range(4):
                packed = jnp.zeros((8, LANES), F32)
                for k in range(32):
                    value = edges[j, side, 32 * g + k].astype(F32)
                    value = pltpu.roll(value, 4 * k, 1) if k else value
                    first = 4 * k if side == 0 else (4 * k - 2) % LANES
                    packed = jnp.where((lane == first) | (lane == first + 1), value, packed)
                out[j, g] = packed.astype(BF16)


def pack_edges(phases, coherence):
    count, rows, _ = phases.shape
    small = jax.ShapeDtypeStruct((2, count // 32, rows, LANES), BF16)
    return pl.pallas_call(
        pack_kernel,
        in_specs=[HBM, HBM],
        out_specs=[VMEM, VMEM],
        out_shape=[small, small],
        scratch_shapes=[pltpu.VMEM((2, 2, count, rows, LANES), BF16), pltpu.SemaphoreType.DMA((4,))],
        compiler_params=params(60),
        cost_estimate=cost(3e8, 1e6),
        name="pack_edges",
    )(phases, coherence)


def bands_kernel(taps_ref, _, high_ref, low_ref):
    place = lax.broadcasted_iota(jnp.int32, (2 * LANES, LANES), 0)
    place = jnp.where(place >= LANES + 64, place - 2 * LANES, place)
    tap = place - lax.broadcasted_iota(jnp.int32, (2 * LANES, LANES), 1) + 2
    for a in range(3):
        band = jnp.zeros((2 * LANES, LANES), F32)
        for b in range(5):
            band = jnp.where(tap == b, taps_ref[a, b], band)
        high = band.astype(BF16)
        high_ref[:, a * LANES : (a + 1) * LANES] = high
        low_ref[:, a * LANES : (a + 1) * LANES] = (band - high.astype(F32)).astype(BF16)

def bands(taps, after):
    shape = jax.ShapeDtypeStruct((2 * LANES, 3 * LANES), BF16)
    return pl.pallas_call(bands_kernel, in_specs=[SMEM, ANY], out_specs=[VMEM, VMEM], out_shape=[shape, shape],
        compiler_params=params(), cost_estimate=cost(3e8,1e5), name="bands")(taps, after)


def expand_kernel(left_ref, right_ref, phase_out, coh_out):
    lane = lax.broadcasted_iota(jnp.int32, (4, 8, LANES), 2)
    from_left = (lane & 3) >= 2
    for j, out in ((0, phase_out), (1, coh_out)):
        both = jnp.where(from_left, left_ref[j].astype(F32), right_ref[j].astype(F32))
        for k in range(32):
            out[:, k] = (pltpu.roll(both, (LANES - 4 * k) % LANES, 2) if k else both).astype(BF16)

def expand(left, right):
    shape = jax.ShapeDtypeStruct((4, 32, 8, LANES), BF16)
    out = pl.pallas_call(expand_kernel, in_specs=[VMEM, VMEM], out_specs=[VMEM, VMEM], out_shape=[shape, shape],
        compiler_params=params(), cost_estimate=cost(5e8,1e5), name="expand")(left, right)
    return [o.reshape(128, 8, LANES) for o in out]


def filter_kernel(step, m, me_ref, high_ref, low_ref, phase_ref, coh_ref, phase_edge_ref, coh_edge_ref, out_ref, scratch):
    block = me_ref[0] ^ step
    count = phase_ref.shape[0]
    blocks = phase_ref.shape[2] // LANES
    group = m // 8
    lane = lax.broadcasted_iota(jnp.int32, (1, 1, LANES), 2)
    left_here = jnp.where(block == 0, LANES, 64)
    right_here = jnp.where(block == blocks - 1, 0, 64)
    use_left = lane >= left_here
    use_right = lane < right_here
    row = lax.broadcasted_iota(jnp.int32, (group, 8, LANES), 1)

    def column(index):
        return pl.ds(pl.multiple_of(index * LANES, LANES), LANES)
    here, before, after = column(block), column(jnp.maximum(block - 1, 0)), column(jnp.minimum(block + 1, blocks - 1))

    def body(i, carry):
        at = pl.ds(i * group, group)
        def edge(ref, edge_ref):
            return jnp.where(use_left, ref[at, :, before], jnp.where(use_right, ref[at, :, after], edge_ref[at]))
        def flat(x):
            return x.reshape(m, LANES)
        phase = jnp.concatenate([flat(phase_ref[at, :, here]), flat(edge(phase_ref, phase_edge_ref))], axis=1)
        coh = jnp.concatenate([flat(coh_ref[at, :, here]), flat(edge(coh_ref, coh_edge_ref))], axis=1)
        product = phase.astype(F32) * coh.astype(F32)
        major = product.astype(BF16)
        minor = (product - major.astype(F32)).astype(BF16)
        high, low = high_ref[...], low_ref[...]
        den = jnp.dot(jnp.concatenate([coh, coh], axis=1), jnp.concatenate([high, low], axis=0), preferred_element_type=F32)
        num = jnp.dot(jnp.concatenate([major, minor, major], axis=1), jnp.concatenate([high, high, low], axis=0), preferred_element_type=F32)
        def vertical(parts):
            p = [parts[:, a * LANES : (a + 1) * LANES].reshape(group, 8, LANES) for a in range(3)]
            down = jnp.where(row == 0, 0.0, pltpu.roll(p[0], 1, 1))
            up = jnp.where(row == 7, 0.0, pltpu.roll(p[2], 7, 1))
            return p[1] + down + up
        bottom = vertical(den)
        inverse = pl.reciprocal(bottom, approx=True)
        inverse = inverse * (2.0 - bottom * inverse)
        result = vertical(num) * inverse
        scratch[pl.ds(pl.multiple_of(i * m, m), m), :] = result.reshape(m, LANES)
        return carry
    if count // group == 1:
        body(0, 0)
    else:
        lax.fori_loop(0, count // group, body, 0)
    for r in range(8):
        out_ref[:, r * LANES : (r + 1) * LANES] = scratch[pl.ds(r, count, stride=8), :].astype(BF16)

def filter_block(step, me, bands, phases, coherence, phase_edge, coh_edge):
    count, rows, _ = phases.shape
    return pl.pallas_call(
        functools.partial(filter_kernel, step, SIZE),
        in_specs=[SMEM] + [VMEM] * 6,
        out_specs=VMEM,
        out_shape=jax.ShapeDtypeStruct((count, rows * LANES), BF16),
        scratch_shapes=[pltpu.VMEM((count * rows, LANES), F32)],
        compiler_params=params(),
        cost_estimate=cost(3e8,1e5),
        name="filter",
    )(me, *bands, phases, coherence, phase_edge, coh_edge)


def network_kernel(pairs_ref, triplets_ref, member_ref, dates_ref, first):
    count = pairs_ref.shape[1]
    triplet_count = triplets_ref.shape[1]
    date_count = dates_ref.shape[1]
    pairs = jnp.concatenate([pairs_ref[...], jnp.zeros((6, count), jnp.int32)], axis=0).T
    triplets = jnp.concatenate([triplets_ref[...], jnp.zeros((5, triplet_count), jnp.int32)], axis=0).T
    for at in range(0, count, LANES):
        column = lax.broadcasted_iota(jnp.int32, (LANES, date_count), 1)
        block = pairs[at : at + LANES]
        value = jnp.where(column == block[:, 1:2], 1.0, 0.0) - jnp.where(column == block[:, 0:1], 1.0, 0.0)
        first[at : at + LANES, :] = value.astype(BF16)
    for at in range(0, triplet_count, LANES):
        column = lax.broadcasted_iota(jnp.int32, (LANES, count), 1)
        block = triplets[at : at + LANES]
        value = (
            jnp.where(column == block[:, 0:1], 1.0, 0.0)
            + jnp.where(column == block[:, 1:2], 1.0, 0.0)
            - jnp.where(column == block[:, 2:3], 1.0, 0.0)
        )
        member_ref[at : at + LANES, :] = value.astype(BF16)
    dates_ref[...] = jnp.dot(member_ref[...], first[...], preferred_element_type=F32).astype(BF16)


def network(date_pairs, triplets, dates):
    count = date_pairs.shape[0]
    triplet_count = triplets.shape[0]
    return pl.pallas_call(
        network_kernel,
        in_specs=[VMEM, VMEM],
        out_specs=[VMEM, VMEM],
        out_shape=[
            jax.ShapeDtypeStruct((triplet_count, count), BF16),
            jax.ShapeDtypeStruct((triplet_count, dates), BF16),
        ],
        scratch_shapes=[pltpu.VMEM((count, dates), BF16)],
        compiler_params=params(),
        cost_estimate=cost(2e9,1e6),
        name="network",
    )(date_pairs.T, triplets.T)


def piece(me, step, matrix_ref, rows, share):
    source = pl.multiple_of((me ^ step) * share, share)
    return matrix_ref[rows, pl.ds(source, share)]


def early_kernel(steps, me_ref, inverse_ref, member_ref, *refs):
    pieces, total_ref = refs[:-1], refs[-1]
    me = me_ref[0]
    share = pieces[0].shape[0]
    dates = inverse_ref.shape[0]
    for at in range(0, total_ref.shape[0], dates):
        matrix_ref, rows = (inverse_ref, pl.ds(0, dates)) if at == 0 else (member_ref, pl.ds(at - dates, dates))
        total = None
        for j in range(0, len(steps), 2):
            left = jnp.concatenate([piece(me, s, matrix_ref, rows, share) for s in steps[j : j + 2]], axis=1)
            right = jnp.concatenate([p[...] for p in pieces[j : j + 2]], axis=0)
            part = jnp.dot(left, right, preferred_element_type=F32)
            total = part if total is None else total + part
        total_ref[pl.ds(at, dates), :] = total


def early_sum(steps, me, inverse, member, pieces):
    rows = inverse.shape[0] + member.shape[0]
    width = pieces[0].shape[1]
    return pl.pallas_call(
        functools.partial(early_kernel, steps),
        in_specs=[SMEM] + [VMEM] * (2 + len(pieces)),
        out_specs=VMEM,
        out_shape=jax.ShapeDtypeStruct((rows, width), F32),
        compiler_params=params(),
        cost_estimate=cost(5e8,1e5),
        name="early_sum",
    )(me, inverse, member, *pieces)


def late_kernel(steps, me_ref, inverse_ref, member_ref, dates_ref, total_ref, *refs):
    count = len(steps)
    pieces = refs[:count]
    disp_hbm, closure_hbm, disp, closure, rounded, spread, sems = refs[count:]
    me = me_ref[0]
    share = pieces[0].shape[0]
    dates = inverse_ref.shape[0]
    rows = disp.shape[1]
    right = jnp.concatenate([p[...] for p in pieces], axis=0)
    chunk = 128

    def times(matrix_ref, at):
        left = jnp.concatenate([piece(me, s, matrix_ref, pl.ds(at, chunk), share) for s in steps], axis=1)
        return jnp.dot(left, right, preferred_element_type=F32)

    def regroup(slot, value, out, at):
        for r in range(rows):
            spread[slot, pl.ds(r, chunk, stride=rows), :] = value[:, r * LANES : (r + 1) * LANES]
        out[pl.ds(at, chunk)] = spread[slot].reshape(chunk, rows, LANES).astype(BF16)

    copies = []

    def send(out, hbm, at):
        copy = pltpu.make_async_copy(out.at[pl.ds(at, chunk)], hbm.at[pl.ds(at, chunk)], sems.at[len(copies)])
        copy.start()
        copies.append(copy)

    for at in range(0, dates, chunk):
        value = (total_ref[pl.ds(at, chunk), :] + times(inverse_ref, at)).astype(BF16)
        rounded[pl.ds(at, chunk), :] = value
        regroup(len(copies) % 2, value.astype(F32), disp, at)
        send(disp, disp_hbm, at)
    for at in range(0, closure.shape[0], chunk):
        value = total_ref[pl.ds(dates + at, chunk), :] + times(member_ref, at)
        value = value - jnp.dot(dates_ref[pl.ds(at, chunk), :], rounded[...], preferred_element_type=F32)
        regroup(len(copies) % 2, value, closure, at)
        send(closure, closure_hbm, at)
    for copy in copies:
        copy.wait()


def late_sum(steps, me, inverse, member, dates_matrix, total, pieces, rows):
    dates = inverse.shape[0]
    triplet_count = member.shape[0]
    width = pieces[0].shape[1]
    outs = [(dates, rows, LANES), (triplet_count, rows, LANES)]
    return pl.pallas_call(
        functools.partial(late_kernel, steps),
        in_specs=[SMEM] + [VMEM] * (4 + len(pieces)),
        out_specs=[HBM, HBM],
        out_shape=[jax.ShapeDtypeStruct(shape, BF16) for shape in outs],
        scratch_shapes=[
            pltpu.VMEM(outs[0], BF16),
            pltpu.VMEM(outs[1], BF16),
            pltpu.VMEM((dates, width), BF16),
            pltpu.VMEM((2, 128 * rows, LANES), F32),
            pltpu.SemaphoreType.DMA(((dates + triplet_count) // 128,)),
        ],
        compiler_params=params(),
        cost_estimate=cost(3e9,2e6),
        name="late_sum",
    )(me, inverse, member, dates_matrix, total, *pieces)


def per_device(phases, coherence, kernel_taps, inverse, date_pairs, triplets):
    rows = phases.shape[1]
    size = lax.axis_size("img")
    peers = lax.axis_size("ifg")
    me = lax.axis_index("ifg").astype(jnp.int32).reshape(1)
    to_left, to_right = pack_edges(phases, coherence)
    left = lax.ppermute(to_right, "img", [(i, i + 1) for i in range(size - 1)])
    right = lax.ppermute(to_left, "img", [(i + 1, i) for i in range(size - 1)])
    member, dates_matrix = network(date_pairs, triplets, inverse.shape[0])
    tap_bands = bands(kernel_taps, dates_matrix)
    edges = expand(left, right)
    pieces = {}
    for step in ORDER:
        block = filter_block(step, me, tap_bands, phases, coherence, *edges)
        pieces[step] = lax.ppermute(block, "ifg", [(i, i ^ step) for i in range(peers)])
    pieces[0] = filter_block(0, me, tap_bands, phases, coherence, *edges)
    total = early_sum(EARLY, me, inverse, member, [pieces[s] for s in EARLY])
    return tuple(late_sum(LATE, me, inverse, member, dates_matrix, total, [pieces[s] for s in LATE], rows))


def solution(mesh):
    return jax.shard_map(
        per_device,
        mesh=mesh,
        in_specs=(P("ifg", None, "img"), P("ifg", None, "img"), P(), P(), P(), P()),
        out_specs=(P(None, None, ("img", "ifg")), P(None, None, ("img", "ifg"))),
        check_vma=False,
    )
```

```python
import functools

import jax
import jax.numpy as jnp
from jax import lax
from jax.experimental import pallas as pl
from jax.experimental.pallas import tpu as pltpu
from jax.sharding import PartitionSpec as P

LANES = 128
F32 = jnp.float32
BF16 = jnp.bfloat16
VMEM = pl.BlockSpec(memory_space=pltpu.VMEM)
SMEM = pl.BlockSpec(memory_space=pltpu.SMEM)
HBM = pl.BlockSpec(memory_space=pltpu.HBM)
ANY = pl.BlockSpec(memory_space=pl.ANY)
SIZE = 1024
ORDER = (6, 5, 3, 7, 1, 4, 2)
EARLY = (0, 6, 5, 3, 7, 1)
LATE = (4, 2)


def cost(flops, nbytes):
    return pl.CostEstimate(flops=int(flops), bytes_accessed=int(nbytes), transcendentals=0)


def params(mib=16):
    return pltpu.CompilerParams(vmem_limit_bytes=mib * 1024 * 1024)


def pack_kernel(phase_hbm, coh_hbm, left_out, right_out, edges, sems):
    width = phase_hbm.shape[2]
    copies = []
    for j, hbm in enumerate((phase_hbm, coh_hbm)):
        for side, at in ((0, 0), (1, width - LANES)):
            copies.append(pltpu.make_async_copy(hbm.at[:, :, pl.ds(at, LANES)], edges.at[j, side], sems.at[2 * j + side]))
    for copy in copies:
        copy.start()
    lane = lax.broadcasted_iota(jnp.int32, (8, LANES), 1)
    for j in range(2):
        for side, out in ((0, left_out), (1, right_out)):
            copies[2 * j + side].wait()
            for g in range(4):
                packed = jnp.zeros((8, LANES), F32)
                for k in range(32):
                    value = edges[j, side, 32 * g + k].astype(F32)
                    value = pltpu.roll(value, 4 * k, 1) if k else value
                    first = 4 * k if side == 0 else (4 * k - 2) % LANES
                    packed = jnp.where((lane == first) | (lane == first + 1), value, packed)
                out[j, g] = packed.astype(BF16)


def pack_edges(phases, coherence):
    count, rows, _ = phases.shape
    small = jax.ShapeDtypeStruct((2, count // 32, rows, LANES), BF16)
    return pl.pallas_call(
        pack_kernel,
        in_specs=[HBM, HBM],
        out_specs=[VMEM, VMEM],
        out_shape=[small, small],
        scratch_shapes=[pltpu.VMEM((2, 2, count, rows, LANES), BF16), pltpu.SemaphoreType.DMA((4,))],
        compiler_params=params(60),
        cost_estimate=cost(3e8, 1e6),
        name="pack_edges",
    )(phases, coherence)


def bands_kernel(taps_ref, _, high_ref, low_ref):
    place = lax.broadcasted_iota(jnp.int32, (2 * LANES, LANES), 0)
    place = jnp.where(place >= LANES + 64, place - 2 * LANES, place)
    tap = place - lax.broadcasted_iota(jnp.int32, (2 * LANES, LANES), 1) + 2
    for a in range(3):
        band = jnp.zeros((2 * LANES, LANES), F32)
        for b in range(5):
            band = jnp.where(tap == b, taps_ref[a, b], band)
        high = band.astype(BF16)
        high_ref[:, a * LANES : (a + 1) * LANES] = high
        low_ref[:, a * LANES : (a + 1) * LANES] = (band - high.astype(F32)).astype(BF16)

def bands(taps, after):
    shape = jax.ShapeDtypeStruct((2 * LANES, 3 * LANES), BF16)
    return pl.pallas_call(bands_kernel, in_specs=[SMEM, ANY], out_specs=[VMEM, VMEM], out_shape=[shape, shape],
        compiler_params=params(), cost_estimate=cost(3e8,1e5), name="bands")(taps, after)


def expand_kernel(left_ref, right_ref, phase_out, coh_out):
    lane = lax.broadcasted_iota(jnp.int32, (4, 8, LANES), 2)
    from_left = (lane & 3) >= 2
    for j, out in ((0, phase_out), (1, coh_out)):
        both = jnp.where(from_left, left_ref[j].astype(F32), right_ref[j].astype(F32))
        for k in range(32):
            out[:, k] = (pltpu.roll(both, (LANES - 4 * k) % LANES, 2) if k else both).astype(BF16)

def expand(left, right):
    shape = jax.ShapeDtypeStruct((4, 32, 8, LANES), BF16)
    out = pl.pallas_call(expand_kernel, in_specs=[VMEM, VMEM], out_specs=[VMEM, VMEM], out_shape=[shape, shape],
        compiler_params=params(), cost_estimate=cost(5e8,1e5), name="expand")(left, right)
    return [o.reshape(128, 8, LANES) for o in out]


def filter_kernel(step, m, me_ref, high_ref, low_ref, phase_ref, coh_ref, phase_edge_ref, coh_edge_ref, out_ref, scratch):
    block = me_ref[0] ^ step
    count = phase_ref.shape[0]
    blocks = phase_ref.shape[2] // LANES
    group = m // 8
    lane = lax.broadcasted_iota(jnp.int32, (1, 1, LANES), 2)
    left_here = jnp.where(block == 0, LANES, 64)
    right_here = jnp.where(block == blocks - 1, 0, 64)
    use_left = lane >= left_here
    use_right = lane < right_here
    row = lax.broadcasted_iota(jnp.int32, (group, 8, LANES), 1)

    def column(index):
        return pl.ds(pl.multiple_of(index * LANES, LANES), LANES)
    here, before, after = column(block), column(jnp.maximum(block - 1, 0)), column(jnp.minimum(block + 1, blocks - 1))

    def body(i, carry):
        at = pl.ds(i * group, group)
        def edge(ref, edge_ref):
            return jnp.where(use_left, ref[at, :, before], jnp.where(use_right, ref[at, :, after], edge_ref[at]))
        def flat(x):
            return x.reshape(m, LANES)
        phase = jnp.concatenate([flat(phase_ref[at, :, here]), flat(edge(phase_ref, phase_edge_ref))], axis=1)
        coh = jnp.concatenate([flat(coh_ref[at, :, here]), flat(edge(coh_ref, coh_edge_ref))], axis=1)
        product = phase.astype(F32) * coh.astype(F32)
        major = product.astype(BF16)
        minor = (product - major.astype(F32)).astype(BF16)
        high, low = high_ref[...], low_ref[...]
        den = jnp.dot(jnp.concatenate([coh, coh], axis=1), jnp.concatenate([high, low], axis=0), preferred_element_type=F32)
        num = jnp.dot(jnp.concatenate([major, minor, major], axis=1), jnp.concatenate([high, high, low], axis=0), preferred_element_type=F32)
        def vertical(parts):
            p = [parts[:, a * LANES : (a + 1) * LANES].reshape(group, 8, LANES) for a in range(3)]
            down = jnp.where(row == 0, 0.0, pltpu.roll(p[0], 1, 1))
            up = jnp.where(row == 7, 0.0, pltpu.roll(p[2], 7, 1))
            return p[1] + down + up
        bottom = vertical(den)
        inverse = pl.reciprocal(bottom, approx=True)
        inverse = inverse * (2.0 - bottom * inverse)
        result = vertical(num) * inverse
        scratch[pl.ds(pl.multiple_of(i * m, m), m), :] = result.reshape(m, LANES)
        return carry
    if count // group == 1:
        body(0, 0)
    else:
        lax.fori_loop(0, count // group, body, 0)
    for r in range(8):
        out_ref[:, r * LANES : (r + 1) * LANES] = scratch[pl.ds(r, count, stride=8), :].astype(BF16)

def filter_block(step, me, bands, phases, coherence, phase_edge, coh_edge):
    count, rows, _ = phases.shape
    return pl.pallas_call(
        functools.partial(filter_kernel, step, SIZE),
        in_specs=[SMEM] + [VMEM] * 6,
        out_specs=VMEM,
        out_shape=jax.ShapeDtypeStruct((count, rows * LANES), BF16),
        scratch_shapes=[pltpu.VMEM((count * rows, LANES), F32)],
        compiler_params=params(),
        cost_estimate=cost(3e8,1e5),
        name="filter",
    )(me, *bands, phases, coherence, phase_edge, coh_edge)


def network_kernel(pairs_ref, triplets_ref, member_ref, dates_ref, first):
    count = pairs_ref.shape[1]
    triplet_count = triplets_ref.shape[1]
    date_count = dates_ref.shape[1]
    pairs = jnp.concatenate([pairs_ref[...], jnp.zeros((6, count), jnp.int32)], axis=0).T
    triplets = jnp.concatenate([triplets_ref[...], jnp.zeros((5, triplet_count), jnp.int32)], axis=0).T
    for at in range(0, count, LANES):
        column = lax.broadcasted_iota(jnp.int32, (LANES, date_count), 1)
        block = pairs[at : at + LANES]
        value = jnp.where(column == block[:, 1:2], 1.0, 0.0) - jnp.where(column == block[:, 0:1], 1.0, 0.0)
        first[at : at + LANES, :] = value.astype(BF16)
    for at in range(0, triplet_count, LANES):
        column = lax.broadcasted_iota(jnp.int32, (LANES, count), 1)
        block = triplets[at : at + LANES]
        value = (
            jnp.where(column == block[:, 0:1], 1.0, 0.0)
            + jnp.where(column == block[:, 1:2], 1.0, 0.0)
            - jnp.where(column == block[:, 2:3], 1.0, 0.0)
        )
        member_ref[at : at + LANES, :] = value.astype(BF16)
    dates_ref[...] = jnp.dot(member_ref[...], first[...], preferred_element_type=F32).astype(BF16)


def network(date_pairs, triplets, dates):
    count = date_pairs.shape[0]
    triplet_count = triplets.shape[0]
    return pl.pallas_call(
        network_kernel,
        in_specs=[VMEM, VMEM],
        out_specs=[VMEM, VMEM],
        out_shape=[
            jax.ShapeDtypeStruct((triplet_count, count), BF16),
            jax.ShapeDtypeStruct((triplet_count, dates), BF16),
        ],
        scratch_shapes=[pltpu.VMEM((count, dates), BF16)],
        compiler_params=params(),
        cost_estimate=cost(2e9,1e6),
        name="network",
    )(date_pairs.T, triplets.T)


def piece(me, step, matrix_ref, rows, share):
    source = pl.multiple_of((me ^ step) * share, share)
    return matrix_ref[rows, pl.ds(source, share)]


def early_kernel(steps, me_ref, inverse_ref, member_ref, *refs):
    pieces, total_ref = refs[:-1], refs[-1]
    me = me_ref[0]
    share = pieces[0].shape[0]
    dates = inverse_ref.shape[0]
    for at in range(0, total_ref.shape[0], dates):
        matrix_ref, rows = (inverse_ref, pl.ds(0, dates)) if at == 0 else (member_ref, pl.ds(at - dates, dates))
        total = None
        for j in range(0, len(steps), 2):
            left = jnp.concatenate([piece(me, s, matrix_ref, rows, share) for s in steps[j : j + 2]], axis=1)
            right = jnp.concatenate([p[...] for p in pieces[j : j + 2]], axis=0)
            part = jnp.dot(left, right, preferred_element_type=F32)
            total = part if total is None else total + part
        total_ref[pl.ds(at, dates), :] = total


def early_sum(steps, me, inverse, member, pieces):
    rows = inverse.shape[0] + member.shape[0]
    width = pieces[0].shape[1]
    return pl.pallas_call(
        functools.partial(early_kernel, steps),
        in_specs=[SMEM] + [VMEM] * (2 + len(pieces)),
        out_specs=VMEM,
        out_shape=jax.ShapeDtypeStruct((rows, width), F32),
        compiler_params=params(),
        cost_estimate=cost(5e8,1e5),
        name="early_sum",
    )(me, inverse, member, *pieces)


def late_kernel(steps, me_ref, inverse_ref, member_ref, dates_ref, total_ref, *refs):
    count = len(steps)
    pieces = refs[:count]
    disp_hbm, closure_hbm, disp, closure, rounded, spread, sems = refs[count:]
    me = me_ref[0]
    share = pieces[0].shape[0]
    dates = inverse_ref.shape[0]
    rows = disp.shape[1]
    right = jnp.concatenate([p[...] for p in pieces], axis=0)
    chunk = 128

    def times(matrix_ref, at):
        left = jnp.concatenate([piece(me, s, matrix_ref, pl.ds(at, chunk), share) for s in steps], axis=1)
        return jnp.dot(left, right, preferred_element_type=F32)

    def regroup(slot, value, out, at):
        for r in range(rows):
            spread[slot, pl.ds(r, chunk, stride=rows), :] = value[:, r * LANES : (r + 1) * LANES]
        out[pl.ds(at, chunk)] = spread[slot].reshape(chunk, rows, LANES).astype(BF16)

    copies = []

    def send(out, hbm, at):
        copy = pltpu.make_async_copy(out.at[pl.ds(at, chunk)], hbm.at[pl.ds(at, chunk)], sems.at[len(copies)])
        copy.start()
        copies.append(copy)

    for at in range(0, dates, chunk):
        value = (total_ref[pl.ds(at, chunk), :] + times(inverse_ref, at)).astype(BF16)
        rounded[pl.ds(at, chunk), :] = value
        regroup(len(copies) % 2, value.astype(F32), disp, at)
        send(disp, disp_hbm, at)
    for at in range(0, closure.shape[0], chunk):
        value = total_ref[pl.ds(dates + at, chunk), :] + times(member_ref, at)
        value = value - jnp.dot(dates_ref[pl.ds(at, chunk), :], rounded[...], preferred_element_type=F32)
        regroup(len(copies) % 2, value, closure, at)
        send(closure, closure_hbm, at)
    for copy in copies:
        copy.wait()


def late_sum(steps, me, inverse, member, dates_matrix, total, pieces, rows):
    dates = inverse.shape[0]
    triplet_count = member.shape[0]
    width = pieces[0].shape[1]
    outs = [(dates, rows, LANES), (triplet_count, rows, LANES)]
    return pl.pallas_call(
        functools.partial(late_kernel, steps),
        in_specs=[SMEM] + [VMEM] * (4 + len(pieces)),
        out_specs=[HBM, HBM],
        out_shape=[jax.ShapeDtypeStruct(shape, BF16) for shape in outs],
        scratch_shapes=[
            pltpu.VMEM(outs[0], BF16),
            pltpu.VMEM(outs[1], BF16),
            pltpu.VMEM((dates, width), BF16),
            pltpu.VMEM((2, 128 * rows, LANES), F32),
            pltpu.SemaphoreType.DMA(((dates + triplet_count) // 128,)),
        ],
        compiler_params=params(),
        cost_estimate=cost(3e9,2e6),
        name="late_sum",
    )(me, inverse, member, dates_matrix, total, *pieces)


def per_device(phases, coherence, kernel_taps, inverse, date_pairs, triplets):
    rows = phases.shape[1]
    size = lax.axis_size("img")
    peers = lax.axis_size("ifg")
    me = lax.axis_index("ifg").astype(jnp.int32).reshape(1)
    to_left, to_right = pack_edges(phases, coherence)
    left = lax.ppermute(to_right, "img", [(i, i + 1) for i in range(size - 1)])
    right = lax.ppermute(to_left, "img", [(i + 1, i) for i in range(size - 1)])
    member, dates_matrix = network(date_pairs, triplets, inverse.shape[0])
    tap_bands = bands(kernel_taps, dates_matrix)
    edges = expand(left, right)
    pieces = {}
    for step in ORDER:
        block = filter_block(step, me, tap_bands, phases, coherence, *edges)
        pieces[step] = lax.ppermute(block, "ifg", [(i, i ^ step) for i in range(peers)])
    pieces[0] = filter_block(0, me, tap_bands, phases, coherence, *edges)
    total = early_sum(EARLY, me, inverse, member, [pieces[s] for s in EARLY])
    return tuple(late_sum(LATE, me, inverse, member, dates_matrix, total, [pieces[s] for s in LATE], rows))


def solution(mesh):
    return jax.shard_map(
        per_device,
        mesh=mesh,
        in_specs=(P("ifg", None, "img"), P("ifg", None, "img"), P(), P(), P(), P()),
        out_specs=(P(None, None, ("img", "ifg")), P(None, None, ("img", "ifg"))),
        check_vma=False,
    )
```

```python
import functools

import jax
import jax.numpy as jnp
from jax import lax
from jax.experimental import pallas as pl
from jax.experimental.pallas import tpu as pltpu
from jax.sharding import PartitionSpec as P

LANES = 128
F32 = jnp.float32
BF16 = jnp.bfloat16
VMEM = pl.BlockSpec(memory_space=pltpu.VMEM)
SMEM = pl.BlockSpec(memory_space=pltpu.SMEM)
HBM = pl.BlockSpec(memory_space=pltpu.HBM)
ANY = pl.BlockSpec(memory_space=pl.ANY)
SIZE = 1024
ORDER = (6, 5, 3, 7, 1, 4, 2)
EARLY = (0, 6, 5, 3, 7, 1)
LATE = (4, 2)


def cost(flops, nbytes):
    return pl.CostEstimate(flops=int(flops), bytes_accessed=int(nbytes), transcendentals=0)


def params(mib=16):
    return pltpu.CompilerParams(vmem_limit_bytes=mib * 1024 * 1024)


def pack_kernel(phase_hbm, coh_hbm, left_out, right_out, edges, sems):
    width = phase_hbm.shape[2]
    copies = []
    for j, hbm in enumerate((phase_hbm, coh_hbm)):
        for side, at in ((0, 0), (1, width - LANES)):
            copies.append(pltpu.make_async_copy(hbm.at[:, :, pl.ds(at, LANES)], edges.at[j, side], sems.at[2 * j + side]))
    for copy in copies:
        copy.start()
    lane = lax.broadcasted_iota(jnp.int32, (8, LANES), 1)
    for j in range(2):
        for side, out in ((0, left_out), (1, right_out)):
            copies[2 * j + side].wait()
            for g in range(4):
                packed = jnp.zeros((8, LANES), F32)
                for k in range(32):
                    value = edges[j, side, 32 * g + k].astype(F32)
                    value = pltpu.roll(value, 4 * k, 1) if k else value
                    first = 4 * k if side == 0 else (4 * k - 2) % LANES
                    packed = jnp.where((lane == first) | (lane == first + 1), value, packed)
                out[j, g] = packed.astype(BF16)


def pack_edges(phases, coherence):
    count, rows, _ = phases.shape
    small = jax.ShapeDtypeStruct((2, count // 32, rows, LANES), BF16)
    return pl.pallas_call(
        pack_kernel,
        in_specs=[HBM, HBM],
        out_specs=[VMEM, VMEM],
        out_shape=[small, small],
        scratch_shapes=[pltpu.VMEM((2, 2, count, rows, LANES), BF16), pltpu.SemaphoreType.DMA((4,))],
        compiler_params=params(60),
        cost_estimate=cost(3e8, 1e6),
        name="pack_edges",
    )(phases, coherence)


def bands_kernel(taps_ref, high_ref, low_ref):
    place = lax.broadcasted_iota(jnp.int32, (2 * LANES, LANES), 0)
    place = jnp.where(place >= LANES + 64, place - 2 * LANES, place)
    tap = place - lax.broadcasted_iota(jnp.int32, (2 * LANES, LANES), 1) + 2
    for a in range(3):
        band = jnp.zeros((2 * LANES, LANES), F32)
        for b in range(5):
            band = jnp.where(tap == b, taps_ref[a, b], band)
        high = band.astype(BF16)
        high_ref[:, a * LANES : (a + 1) * LANES] = high
        low_ref[:, a * LANES : (a + 1) * LANES] = (band - high.astype(F32)).astype(BF16)

def bands(taps):
    shape = jax.ShapeDtypeStruct((2 * LANES, 3 * LANES), BF16)
    return pl.pallas_call(bands_kernel, in_specs=[SMEM], out_specs=[VMEM, VMEM], out_shape=[shape, shape],
        compiler_params=params(), cost_estimate=cost(2e9,1e6), name="bands")(taps)


def expand_kernel(left_ref, right_ref, phase_out, coh_out):
    lane = lax.broadcasted_iota(jnp.int32, (4, 8, LANES), 2)
    from_left = (lane & 3) >= 2
    for j, out in ((0, phase_out), (1, coh_out)):
        both = jnp.where(from_left, left_ref[j].astype(F32), right_ref[j].astype(F32))
        for k in range(32):
            out[:, k] = (pltpu.roll(both, (LANES - 4 * k) % LANES, 2) if k else both).astype(BF16)

def expand(left, right):
    shape = jax.ShapeDtypeStruct((4, 32, 8, LANES), BF16)
    out = pl.pallas_call(expand_kernel, in_specs=[VMEM, VMEM], out_specs=[VMEM, VMEM], out_shape=[shape, shape],
        compiler_params=params(), cost_estimate=cost(2e9,1e6), name="expand")(left, right)
    return [o.reshape(128, 8, LANES) for o in out]


def filter_kernel(step, m, me_ref, high_ref, low_ref, phase_ref, coh_ref, phase_edge_ref, coh_edge_ref, out_ref, scratch):
    block = me_ref[0] ^ step
    count = phase_ref.shape[0]
    blocks = phase_ref.shape[2] // LANES
    group = m // 8
    lane = lax.broadcasted_iota(jnp.int32, (1, 1, LANES), 2)
    left_here = jnp.where(block == 0, LANES, 64)
    right_here = jnp.where(block == blocks - 1, 0, 64)
    use_left = lane >= left_here
    use_right = lane < right_here
    row = lax.broadcasted_iota(jnp.int32, (group, 8, LANES), 1)

    def column(index):
        return pl.ds(pl.multiple_of(index * LANES, LANES), LANES)
    here, before, after = column(block), column(jnp.maximum(block - 1, 0)), column(jnp.minimum(block + 1, blocks - 1))

    def body(i, carry):
        at = pl.ds(i * group, group)
        def edge(ref, edge_ref):
            return jnp.where(use_left, ref[at, :, before], jnp.where(use_right, ref[at, :, after], edge_ref[at]))
        def flat(x):
            return x.reshape(m, LANES)
        phase = jnp.concatenate([flat(phase_ref[at, :, here]), flat(edge(phase_ref, phase_edge_ref))], axis=1)
        coh = jnp.concatenate([flat(coh_ref[at, :, here]), flat(edge(coh_ref, coh_edge_ref))], axis=1)
        product = phase.astype(F32) * coh.astype(F32)
        major = product.astype(BF16)
        high, low = high_ref[...], low_ref[...]
        den = jnp.dot(jnp.concatenate([coh, coh], axis=1), jnp.concatenate([high, low], axis=0), preferred_element_type=F32)
        num = jnp.dot(jnp.concatenate([major, major], axis=1), jnp.concatenate([high, low], axis=0), preferred_element_type=F32)
        def vertical(parts):
            p = [parts[:, a * LANES : (a + 1) * LANES].reshape(group, 8, LANES) for a in range(3)]
            down = jnp.where(row == 0, 0.0, pltpu.roll(p[0], 1, 1))
            up = jnp.where(row == 7, 0.0, pltpu.roll(p[2], 7, 1))
            return p[1] + down + up
        bottom = vertical(den)
        inverse = pl.reciprocal(bottom, approx=True)
        inverse = inverse * (2.0 - bottom * inverse)
        result = vertical(num) * inverse
        scratch[pl.ds(pl.multiple_of(i * m, m), m), :] = result.reshape(m, LANES)
        return carry
    if count // group == 1:
        body(0, 0)
    else:
        lax.fori_loop(0, count // group, body, 0)
    for r in range(8):
        out_ref[:, r * LANES : (r + 1) * LANES] = scratch[pl.ds(r, count, stride=8), :].astype(BF16)

def filter_block(step, me, bands, phases, coherence, phase_edge, coh_edge):
    count, rows, _ = phases.shape
    return pl.pallas_call(
        functools.partial(filter_kernel, step, SIZE),
        in_specs=[SMEM] + [VMEM] * 6,
        out_specs=VMEM,
        out_shape=jax.ShapeDtypeStruct((count, rows * LANES), BF16),
        scratch_shapes=[pltpu.VMEM((count * rows, LANES), F32)],
        compiler_params=params(),
        cost_estimate=cost(3e8,1e5),
        name="filter",
    )(me, *bands, phases, coherence, phase_edge, coh_edge)


def network_kernel(pairs_ref, triplets_ref, _, member_ref, dates_ref, first):
    count = pairs_ref.shape[1]
    triplet_count = triplets_ref.shape[1]
    date_count = dates_ref.shape[1]
    pairs = jnp.concatenate([pairs_ref[...], jnp.zeros((6, count), jnp.int32)], axis=0).T
    triplets = jnp.concatenate([triplets_ref[...], jnp.zeros((5, triplet_count), jnp.int32)], axis=0).T
    for at in range(0, count, LANES):
        column = lax.broadcasted_iota(jnp.int32, (LANES, date_count), 1)
        block = pairs[at : at + LANES]
        value = jnp.where(column == block[:, 1:2], 1.0, 0.0) - jnp.where(column == block[:, 0:1], 1.0, 0.0)
        first[at : at + LANES, :] = value.astype(BF16)
    for at in range(0, triplet_count, LANES):
        column = lax.broadcasted_iota(jnp.int32, (LANES, count), 1)
        block = triplets[at : at + LANES]
        value = (
            jnp.where(column == block[:, 0:1], 1.0, 0.0)
            + jnp.where(column == block[:, 1:2], 1.0, 0.0)
            - jnp.where(column == block[:, 2:3], 1.0, 0.0)
        )
        member_ref[at : at + LANES, :] = value.astype(BF16)
    dates_ref[...] = jnp.dot(member_ref[...], first[...], preferred_element_type=F32).astype(BF16)


def network(date_pairs, triplets, dates, after):
    count = date_pairs.shape[0]
    triplet_count = triplets.shape[0]
    return pl.pallas_call(
        network_kernel,
        in_specs=[VMEM, VMEM, ANY],
        out_specs=[VMEM, VMEM],
        out_shape=[
            jax.ShapeDtypeStruct((triplet_count, count), BF16),
            jax.ShapeDtypeStruct((triplet_count, dates), BF16),
        ],
        scratch_shapes=[pltpu.VMEM((count, dates), BF16)],
        compiler_params=params(),
        cost_estimate=cost(2e9,1e6),
        name="network",
    )(date_pairs.T, triplets.T, after)


def piece(me, step, matrix_ref, rows, share):
    source = pl.multiple_of((me ^ step) * share, share)
    return matrix_ref[rows, pl.ds(source, share)]


def early_kernel(steps, me_ref, inverse_ref, member_ref, *refs):
    pieces, total_ref = refs[:-1], refs[-1]
    me = me_ref[0]
    share = pieces[0].shape[0]
    dates = inverse_ref.shape[0]
    for at in range(0, total_ref.shape[0], dates):
        matrix_ref, rows = (inverse_ref, pl.ds(0, dates)) if at == 0 else (member_ref, pl.ds(at - dates, dates))
        total = None
        for j in range(0, len(steps), 2):
            left = jnp.concatenate([piece(me, s, matrix_ref, rows, share) for s in steps[j : j + 2]], axis=1)
            right = jnp.concatenate([p[...] for p in pieces[j : j + 2]], axis=0)
            part = jnp.dot(left, right, preferred_element_type=F32)
            total = part if total is None else total + part
        total_ref[pl.ds(at, dates), :] = total


def early_sum(steps, me, inverse, member, pieces):
    rows = inverse.shape[0] + member.shape[0]
    width = pieces[0].shape[1]
    return pl.pallas_call(
        functools.partial(early_kernel, steps),
        in_specs=[SMEM] + [VMEM] * (2 + len(pieces)),
        out_specs=VMEM,
        out_shape=jax.ShapeDtypeStruct((rows, width), F32),
        compiler_params=params(),
        cost_estimate=cost(5e8,1e5),
        name="early_sum",
    )(me, inverse, member, *pieces)


def late_kernel(steps, me_ref, inverse_ref, member_ref, dates_ref, total_ref, *refs):
    count = len(steps)
    pieces = refs[:count]
    disp_hbm, closure_hbm, disp, closure, rounded, spread, sems = refs[count:]
    me = me_ref[0]
    share = pieces[0].shape[0]
    dates = inverse_ref.shape[0]
    rows = disp.shape[1]
    right = jnp.concatenate([p[...] for p in pieces], axis=0)
    chunk = 128

    def times(matrix_ref, at):
        left = jnp.concatenate([piece(me, s, matrix_ref, pl.ds(at, chunk), share) for s in steps], axis=1)
        return jnp.dot(left, right, preferred_element_type=F32)

    def regroup(slot, value, out, at):
        for r in range(rows):
            spread[slot, pl.ds(r, chunk, stride=rows), :] = value[:, r * LANES : (r + 1) * LANES]
        out[pl.ds(at, chunk)] = spread[slot].reshape(chunk, rows, LANES).astype(BF16)

    copies = []

    def send(out, hbm, at):
        copy = pltpu.make_async_copy(out.at[pl.ds(at, chunk)], hbm.at[pl.ds(at, chunk)], sems.at[len(copies)])
        copy.start()
        copies.append(copy)

    for at in range(0, dates, chunk):
        value = (total_ref[pl.ds(at, chunk), :] + times(inverse_ref, at)).astype(BF16)
        rounded[pl.ds(at, chunk), :] = value
        regroup(len(copies) % 2, value.astype(F32), disp, at)
        send(disp, disp_hbm, at)
    for at in range(0, closure.shape[0], chunk):
        value = total_ref[pl.ds(dates + at, chunk), :] + times(member_ref, at)
        value = value - jnp.dot(dates_ref[pl.ds(at, chunk), :], rounded[...], preferred_element_type=F32)
        regroup(len(copies) % 2, value, closure, at)
        send(closure, closure_hbm, at)
    for copy in copies:
        copy.wait()


def late_sum(steps, me, inverse, member, dates_matrix, total, pieces, rows):
    dates = inverse.shape[0]
    triplet_count = member.shape[0]
    width = pieces[0].shape[1]
    outs = [(dates, rows, LANES), (triplet_count, rows, LANES)]
    return pl.pallas_call(
        functools.partial(late_kernel, steps),
        in_specs=[SMEM] + [VMEM] * (4 + len(pieces)),
        out_specs=[HBM, HBM],
        out_shape=[jax.ShapeDtypeStruct(shape, BF16) for shape in outs],
        scratch_shapes=[
            pltpu.VMEM(outs[0], BF16),
            pltpu.VMEM(outs[1], BF16),
            pltpu.VMEM((dates, width), BF16),
            pltpu.VMEM((2, 128 * rows, LANES), F32),
            pltpu.SemaphoreType.DMA(((dates + triplet_count) // 128,)),
        ],
        compiler_params=params(),
        cost_estimate=cost(3e9,2e6),
        name="late_sum",
    )(me, inverse, member, dates_matrix, total, *pieces)


def per_device(phases, coherence, kernel_taps, inverse, date_pairs, triplets):
    rows = phases.shape[1]
    size = lax.axis_size("img")
    peers = lax.axis_size("ifg")
    me = lax.axis_index("ifg").astype(jnp.int32).reshape(1)
    to_left, to_right = pack_edges(phases, coherence)
    left = lax.ppermute(to_right, "img", [(i, i + 1) for i in range(size - 1)])
    right = lax.ppermute(to_left, "img", [(i + 1, i) for i in range(size - 1)])
    tap_bands = bands(kernel_taps)
    edges = expand(left, right)
    pieces = {}
    for step in ORDER:
        block = filter_block(step, me, tap_bands, phases, coherence, *edges)
        pieces[step] = lax.ppermute(block, "ifg", [(i, i ^ step) for i in range(peers)])
    member, dates_matrix = network(date_pairs, triplets, inverse.shape[0], block)
    pieces[0] = filter_block(0, me, tap_bands, phases, coherence, *edges)
    total = early_sum(EARLY, me, inverse, member, [pieces[s] for s in EARLY])
    return tuple(late_sum(LATE, me, inverse, member, dates_matrix, total, [pieces[s] for s in LATE], rows))


def solution(mesh):
    return jax.shard_map(
        per_device,
        mesh=mesh,
        in_specs=(P("ifg", None, "img"), P("ifg", None, "img"), P(), P(), P(), P()),
        out_specs=(P(None, None, ("img", "ifg")), P(None, None, ("img", "ifg"))),
        check_vma=False,
    )
```

```python
import functools

import jax
import jax.numpy as jnp
from jax import lax
from jax.experimental import pallas as pl
from jax.experimental.pallas import tpu as pltpu
from jax.sharding import PartitionSpec as P

LANES = 128
F32 = jnp.float32
BF16 = jnp.bfloat16
VMEM = pl.BlockSpec(memory_space=pltpu.VMEM)
SMEM = pl.BlockSpec(memory_space=pltpu.SMEM)
HBM = pl.BlockSpec(memory_space=pltpu.HBM)
ANY = pl.BlockSpec(memory_space=pl.ANY)
SIZE = 1024
ORDER = (6, 5, 3, 7, 1, 4, 2)
EARLY = (0, 6, 5, 3, 7, 1)
LATE = (4, 2)


def cost(flops, nbytes):
    return pl.CostEstimate(flops=int(flops), bytes_accessed=int(nbytes), transcendentals=0)


def params(mib=16):
    return pltpu.CompilerParams(vmem_limit_bytes=mib * 1024 * 1024)


def pack_kernel(phase_hbm, coh_hbm, left_out, right_out, edges, sems):
    width = phase_hbm.shape[2]
    copies = []
    for j, hbm in enumerate((phase_hbm, coh_hbm)):
        for side, at in ((0, 0), (1, width - LANES)):
            copies.append(pltpu.make_async_copy(hbm.at[:, :, pl.ds(at, LANES)], edges.at[j, side], sems.at[2 * j + side]))
    for copy in copies:
        copy.start()
    lane = lax.broadcasted_iota(jnp.int32, (8, LANES), 1)
    for j in range(2):
        for side, out in ((0, left_out), (1, right_out)):
            copies[2 * j + side].wait()
            for g in range(4):
                packed = jnp.zeros((8, LANES), F32)
                for k in range(32):
                    value = edges[j, side, 32 * g + k].astype(F32)
                    value = pltpu.roll(value, 4 * k, 1) if k else value
                    first = 4 * k if side == 0 else (4 * k - 2) % LANES
                    packed = jnp.where((lane == first) | (lane == first + 1), value, packed)
                out[j, g] = packed.astype(BF16)


def pack_edges(phases, coherence):
    count, rows, _ = phases.shape
    small = jax.ShapeDtypeStruct((2, count // 32, rows, LANES), BF16)
    return pl.pallas_call(
        pack_kernel,
        in_specs=[HBM, HBM],
        out_specs=[VMEM, VMEM],
        out_shape=[small, small],
        scratch_shapes=[pltpu.VMEM((2, 2, count, rows, LANES), BF16), pltpu.SemaphoreType.DMA((4,))],
        compiler_params=params(60),
        cost_estimate=cost(3e8, 1e6),
        name="pack_edges",
    )(phases, coherence)


def bands_kernel(taps_ref, band_ref):
    place = lax.broadcasted_iota(jnp.int32, (2 * LANES, LANES), 0)
    place = jnp.where(place >= LANES + 64, place - 2 * LANES, place)
    tap = place - lax.broadcasted_iota(jnp.int32, (2 * LANES, LANES), 1) + 2
    for a in range(3):
        band = jnp.zeros((2 * LANES, LANES), F32)
        for b in range(5):
            band = jnp.where(tap == b, taps_ref[a, b], band)
        band_ref[:, a * LANES : (a + 1) * LANES] = band.astype(BF16)

def bands(taps):
    shape = jax.ShapeDtypeStruct((2 * LANES, 3 * LANES), BF16)
    return pl.pallas_call(bands_kernel, in_specs=[SMEM], out_specs=VMEM, out_shape=shape,
        compiler_params=params(), cost_estimate=cost(2e9,1e6), name="bands")(taps)


def expand_kernel(left_ref, right_ref, phase_out, coh_out):
    lane = lax.broadcasted_iota(jnp.int32, (4, 8, LANES), 2)
    from_left = (lane & 3) >= 2
    for j, out in ((0, phase_out), (1, coh_out)):
        both = jnp.where(from_left, left_ref[j].astype(F32), right_ref[j].astype(F32))
        for k in range(32):
            out[:, k] = (pltpu.roll(both, (LANES - 4 * k) % LANES, 2) if k else both).astype(BF16)

def expand(left, right):
    shape = jax.ShapeDtypeStruct((4, 32, 8, LANES), BF16)
    out = pl.pallas_call(expand_kernel, in_specs=[VMEM, VMEM], out_specs=[VMEM, VMEM], out_shape=[shape, shape],
        compiler_params=params(), cost_estimate=cost(2e9,1e6), name="expand")(left, right)
    return [o.reshape(128, 8, LANES) for o in out]


def filter_kernel(step, m, me_ref, band_ref, phase_ref, coh_ref, phase_edge_ref, coh_edge_ref, out_ref, scratch):
    block = me_ref[0] ^ step
    count = phase_ref.shape[0]
    blocks = phase_ref.shape[2] // LANES
    group = m // 8
    lane = lax.broadcasted_iota(jnp.int32, (1, 1, LANES), 2)
    left_here = jnp.where(block == 0, LANES, 64)
    right_here = jnp.where(block == blocks - 1, 0, 64)
    use_left = lane >= left_here
    use_right = lane < right_here
    row = lax.broadcasted_iota(jnp.int32, (group, 8, LANES), 1)

    def column(index):
        return pl.ds(pl.multiple_of(index * LANES, LANES), LANES)
    here, before, after = column(block), column(jnp.maximum(block - 1, 0)), column(jnp.minimum(block + 1, blocks - 1))

    def body(i, carry):
        at = pl.ds(i * group, group)
        def edge(ref, edge_ref):
            return jnp.where(use_left, ref[at, :, before], jnp.where(use_right, ref[at, :, after], edge_ref[at]))
        def flat(x):
            return x.reshape(m, LANES)
        phase = jnp.concatenate([flat(phase_ref[at, :, here]), flat(edge(phase_ref, phase_edge_ref))], axis=1)
        coh = jnp.concatenate([flat(coh_ref[at, :, here]), flat(edge(coh_ref, coh_edge_ref))], axis=1)
        product = phase.astype(F32) * coh.astype(F32)
        major = product.astype(BF16)
        minor = (product - major.astype(F32)).astype(BF16)
        high = band_ref[...]
        den = jnp.dot(coh, high, preferred_element_type=F32)
        num = jnp.dot(jnp.concatenate([major, minor], axis=1), jnp.concatenate([high, high], axis=0), preferred_element_type=F32)
        def vertical(parts):
            p = [parts[:, a * LANES : (a + 1) * LANES].reshape(group, 8, LANES) for a in range(3)]
            down = jnp.where(row == 0, 0.0, pltpu.roll(p[0], 1, 1))
            up = jnp.where(row == 7, 0.0, pltpu.roll(p[2], 7, 1))
            return p[1] + down + up
        bottom = vertical(den)
        inverse = pl.reciprocal(bottom, approx=True)
        inverse = inverse * (2.0 - bottom * inverse)
        result = vertical(num) * inverse
        scratch[pl.ds(pl.multiple_of(i * m, m), m), :] = result.reshape(m, LANES)
        return carry
    if count // group == 1:
        body(0, 0)
    else:
        lax.fori_loop(0, count // group, body, 0)
    for r in range(8):
        out_ref[:, r * LANES : (r + 1) * LANES] = scratch[pl.ds(r, count, stride=8), :].astype(BF16)

def filter_block(step, me, bands, phases, coherence, phase_edge, coh_edge):
    count, rows, _ = phases.shape
    return pl.pallas_call(
        functools.partial(filter_kernel, step, SIZE),
        in_specs=[SMEM] + [VMEM] * 5,
        out_specs=VMEM,
        out_shape=jax.ShapeDtypeStruct((count, rows * LANES), BF16),
        scratch_shapes=[pltpu.VMEM((count * rows, LANES), F32)],
        compiler_params=params(),
        cost_estimate=cost(3e8,1e5),
        name="filter",
    )(me, bands, phases, coherence, phase_edge, coh_edge)


def network_kernel(pairs_ref, triplets_ref, _, member_ref, dates_ref, first):
    count = pairs_ref.shape[1]
    triplet_count = triplets_ref.shape[1]
    date_count = dates_ref.shape[1]
    pairs = jnp.concatenate([pairs_ref[...], jnp.zeros((6, count), jnp.int32)], axis=0).T
    triplets = jnp.concatenate([triplets_ref[...], jnp.zeros((5, triplet_count), jnp.int32)], axis=0).T
    for at in range(0, count, LANES):
        column = lax.broadcasted_iota(jnp.int32, (LANES, date_count), 1)
        block = pairs[at : at + LANES]
        value = jnp.where(column == block[:, 1:2], 1.0, 0.0) - jnp.where(column == block[:, 0:1], 1.0, 0.0)
        first[at : at + LANES, :] = value.astype(BF16)
    for at in range(0, triplet_count, LANES):
        column = lax.broadcasted_iota(jnp.int32, (LANES, count), 1)
        block = triplets[at : at + LANES]
        value = (
            jnp.where(column == block[:, 0:1], 1.0, 0.0)
            + jnp.where(column == block[:, 1:2], 1.0, 0.0)
            - jnp.where(column == block[:, 2:3], 1.0, 0.0)
        )
        member_ref[at : at + LANES, :] = value.astype(BF16)
    dates_ref[...] = jnp.dot(member_ref[...], first[...], preferred_element_type=F32).astype(BF16)


def network(date_pairs, triplets, dates, after):
    count = date_pairs.shape[0]
    triplet_count = triplets.shape[0]
    return pl.pallas_call(
        network_kernel,
        in_specs=[VMEM, VMEM, ANY],
        out_specs=[VMEM, VMEM],
        out_shape=[
            jax.ShapeDtypeStruct((triplet_count, count), BF16),
            jax.ShapeDtypeStruct((triplet_count, dates), BF16),
        ],
        scratch_shapes=[pltpu.VMEM((count, dates), BF16)],
        compiler_params=params(),
        cost_estimate=cost(2e9,1e6),
        name="network",
    )(date_pairs.T, triplets.T, after)


def piece(me, step, matrix_ref, rows, share):
    source = pl.multiple_of((me ^ step) * share, share)
    return matrix_ref[rows, pl.ds(source, share)]


def early_kernel(steps, me_ref, inverse_ref, member_ref, *refs):
    pieces, total_ref = refs[:-1], refs[-1]
    me = me_ref[0]
    share = pieces[0].shape[0]
    dates = inverse_ref.shape[0]
    for at in range(0, total_ref.shape[0], dates):
        matrix_ref, rows = (inverse_ref, pl.ds(0, dates)) if at == 0 else (member_ref, pl.ds(at - dates, dates))
        total = None
        for j in range(0, len(steps), 2):
            left = jnp.concatenate([piece(me, s, matrix_ref, rows, share) for s in steps[j : j + 2]], axis=1)
            right = jnp.concatenate([p[...] for p in pieces[j : j + 2]], axis=0)
            part = jnp.dot(left, right, preferred_element_type=F32)
            total = part if total is None else total + part
        total_ref[pl.ds(at, dates), :] = total


def early_sum(steps, me, inverse, member, pieces):
    rows = inverse.shape[0] + member.shape[0]
    width = pieces[0].shape[1]
    return pl.pallas_call(
        functools.partial(early_kernel, steps),
        in_specs=[SMEM] + [VMEM] * (2 + len(pieces)),
        out_specs=VMEM,
        out_shape=jax.ShapeDtypeStruct((rows, width), F32),
        compiler_params=params(),
        cost_estimate=cost(5e8,1e5),
        name="early_sum",
    )(me, inverse, member, *pieces)


def late_kernel(steps, me_ref, inverse_ref, member_ref, dates_ref, total_ref, *refs):
    count = len(steps)
    pieces = refs[:count]
    disp_hbm, closure_hbm, disp, closure, rounded, spread, sems = refs[count:]
    me = me_ref[0]
    share = pieces[0].shape[0]
    dates = inverse_ref.shape[0]
    rows = disp.shape[1]
    right = jnp.concatenate([p[...] for p in pieces], axis=0)
    chunk = 128

    def times(matrix_ref, at):
        left = jnp.concatenate([piece(me, s, matrix_ref, pl.ds(at, chunk), share) for s in steps], axis=1)
        return jnp.dot(left, right, preferred_element_type=F32)

    def regroup(slot, value, out, at):
        for r in range(rows):
            spread[slot, pl.ds(r, chunk, stride=rows), :] = value[:, r * LANES : (r + 1) * LANES]
        out[pl.ds(at, chunk)] = spread[slot].reshape(chunk, rows, LANES).astype(BF16)

    copies = []

    def send(out, hbm, at):
        copy = pltpu.make_async_copy(out.at[pl.ds(at, chunk)], hbm.at[pl.ds(at, chunk)], sems.at[len(copies)])
        copy.start()
        copies.append(copy)

    for at in range(0, dates, chunk):
        value = (total_ref[pl.ds(at, chunk), :] + times(inverse_ref, at)).astype(BF16)
        rounded[pl.ds(at, chunk), :] = value
        regroup(len(copies) % 2, value.astype(F32), disp, at)
        send(disp, disp_hbm, at)
    for at in range(0, closure.shape[0], chunk):
        value = total_ref[pl.ds(dates + at, chunk), :] + times(member_ref, at)
        value = value - jnp.dot(dates_ref[pl.ds(at, chunk), :], rounded[...], preferred_element_type=F32)
        regroup(len(copies) % 2, value, closure, at)
        send(closure, closure_hbm, at)
    for copy in copies:
        copy.wait()


def late_sum(steps, me, inverse, member, dates_matrix, total, pieces, rows):
    dates = inverse.shape[0]
    triplet_count = member.shape[0]
    width = pieces[0].shape[1]
    outs = [(dates, rows, LANES), (triplet_count, rows, LANES)]
    return pl.pallas_call(
        functools.partial(late_kernel, steps),
        in_specs=[SMEM] + [VMEM] * (4 + len(pieces)),
        out_specs=[HBM, HBM],
        out_shape=[jax.ShapeDtypeStruct(shape, BF16) for shape in outs],
        scratch_shapes=[
            pltpu.VMEM(outs[0], BF16),
            pltpu.VMEM(outs[1], BF16),
            pltpu.VMEM((dates, width), BF16),
            pltpu.VMEM((2, 128 * rows, LANES), F32),
            pltpu.SemaphoreType.DMA(((dates + triplet_count) // 128,)),
        ],
        compiler_params=params(),
        cost_estimate=cost(3e9,2e6),
        name="late_sum",
    )(me, inverse, member, dates_matrix, total, *pieces)


def per_device(phases, coherence, kernel_taps, inverse, date_pairs, triplets):
    rows = phases.shape[1]
    size = lax.axis_size("img")
    peers = lax.axis_size("ifg")
    me = lax.axis_index("ifg").astype(jnp.int32).reshape(1)
    to_left, to_right = pack_edges(phases, coherence)
    left = lax.ppermute(to_right, "img", [(i, i + 1) for i in range(size - 1)])
    right = lax.ppermute(to_left, "img", [(i + 1, i) for i in range(size - 1)])
    tap_bands = bands(kernel_taps)
    edges = expand(left, right)
    pieces = {}
    for step in ORDER:
        block = filter_block(step, me, tap_bands, phases, coherence, *edges)
        pieces[step] = lax.ppermute(block, "ifg", [(i, i ^ step) for i in range(peers)])
    member, dates_matrix = network(date_pairs, triplets, inverse.shape[0], block)
    pieces[0] = filter_block(0, me, tap_bands, phases, coherence, *edges)
    total = early_sum(EARLY, me, inverse, member, [pieces[s] for s in EARLY])
    return tuple(late_sum(LATE, me, inverse, member, dates_matrix, total, [pieces[s] for s in LATE], rows))


def solution(mesh):
    return jax.shard_map(
        per_device,
        mesh=mesh,
        in_specs=(P("ifg", None, "img"), P("ifg", None, "img"), P(), P(), P(), P()),
        out_specs=(P(None, None, ("img", "ifg")), P(None, None, ("img", "ifg"))),
        check_vma=False,
    )
```
